256 devices in a mesh: span: 16 (over z, core), wall: 16 (over y, x).
Axes of the slice: x: 4, y: 4, z: 8, core: 2. Of those that a mesh axis runs over, the one named last changes fastest.
Arguments:
- residual: float32 [10, 10, 10, 32768], P(None, None, None, ('span', 'wall')), may hold values from -6 to 6
- eig_values: float32 [3, 12, 32768], P(None, None, ('span', 'wall')), may hold values from 0.1 to 20
- eig_vectors: float32 [3, 12, 12, 32768], P(None, None, None, ('span', 'wall')), may hold values from -1.75 to 1.75
- corner_map: int32 [8, 32768], P(None, ('span', 'wall')), may hold values from 0 to 4127, as said below
- stream_links: int32 [2, 16], replicated, may hold values from 0 to 15, as said below
- coarse_inverse: float32 [16, 4128, 4128], P('span', 'wall'), as said below
Outputs:
- preconditioned: float32 [10, 10, 10, 32768], P(None, None, None, ('span', 'wall'))
The draws below stay inside these ranges and needn't reach their ends.
Inputs may be any that keep to these rules, and one draw needn't show every extreme that they name: `corner_map`: entry (c, e) names the coarse vertex at corner c = 4 a + 2 b + d of element e (a, b, d the upper or lower side along span, wall-normal and stream), numbered within the element's span slab; elements of one slab that share a corner name the same vertex, and every vertex of a slab is a corner of some element of it. `stream_links`: each row is a permutation of the slots; row 1 undoes row 0, and following row 1 from any slot visits all 16 slots before it returns. `coarse_inverse`: each slab's matrix is symmetric.
All inputs are finite; a program needn't handle non-finite values.
Results may differ from the reference program's by a relative error of at most 0.000067.
Values sent between devices are 32-bit elements; how exact they have to be, the bound alone decides.
A program may use at most 64 MiB of HBM per device.

```python
import math
import jax
import jax.numpy as jnp
from jax import lax

PTS = 10
EXT = 12
EX = 1
EY = 8
EZ = 16
SLABS = 16
LAYERS = 16
ELEMS = 32768
VERTS = 4128


def stream_order(key):
    return jax.random.permutation(jax.random.fold_in(key, 101), EZ).astype(jnp.int32)


def slot_position(ordering):
    return jnp.zeros((EZ,), jnp.int32).at[ordering].set(jnp.arange(EZ, dtype=jnp.int32))


def draw_stream_links(key, part):
    ordering = stream_order(key)
    position = slot_position(ordering)
    upstream = ordering[jnp.mod(position - 1, EZ)]
    downstream = ordering[jnp.mod(position + 1, EZ)]
    return jnp.stack([upstream, downstream]).astype(jnp.int32)


def shuffle_one(subkey):
    return jax.random.permutation(subkey, VERTS).astype(jnp.int32)


def draw_corner_map(key, part):
    ordering = stream_order(key)
    key = jax.random.fold_in(key, 2)
    position = slot_position(ordering)
    shuffles = jax.vmap(shuffle_one)(jax.random.split(key, SLABS))
    full_shape = (SLABS, LAYERS, EX, EY, EZ)
    slab_index = jnp.broadcast_to(jnp.arange(SLABS, dtype=jnp.int32)[:, None, None, None, None], full_shape)
    layer_index = jnp.arange(LAYERS, dtype=jnp.int32)[None, :, None, None, None]
    span_index = jnp.arange(EX, dtype=jnp.int32)[None, None, :, None, None]
    wall_index = jnp.arange(EY, dtype=jnp.int32)[None, None, None, :, None]
    stream_index = position[None, None, None, None, :]
    corners = []
    for corner in range(8):
        side_span = corner // 4
        side_wall = corner // 2 % 2
        side_stream = corner % 2
        vert_span = span_index + side_span
        vert_wall = layer_index * EY + wall_index + side_wall
        vert_stream = jnp.mod(stream_index + side_stream, EZ)
        drawn = (vert_span * (LAYERS * EY + 1) + vert_wall) * EZ + vert_stream
        drawn = jnp.broadcast_to(drawn, full_shape)
        corners.append(shuffles[slab_index, drawn].reshape(-1))
    return jnp.stack(corners).astype(jnp.int32)


def draw_coarse_inverse(key, part):
    key = jax.random.fold_in(key, 3)

    def noise_of(subkey):
        return jax.random.normal(subkey, (VERTS, VERTS), jnp.float32)

    def one_group(subkey):
        first_key, second_key = jax.random.split(subkey)
        noise = noise_of(first_key)
        scaled = (noise + noise.T) * (0.0045 * VERTS ** (-0.5))
        diagonal = jax.random.uniform(second_key, (VERTS,), jnp.float32, 0.012, 0.03)
        identity = jnp.arange(VERTS)[:, None] == jnp.arange(VERTS)[None, :]
        return jnp.where(identity, diagonal[:, None], scaled)
    return lax.map(one_group, jax.random.split(key, SLABS))


def levels(rng, extent, pieces, least, largest):
    gain = 1.0
    for dim, parts in pieces:
        steps = jax.random.uniform(jax.random.fold_in(jax.random.fold_in(rng, 6), dim), (parts,), jnp.float32, least / len(pieces), largest / len(pieces))
        gain = gain * jnp.repeat(jnp.exp(steps), extent[dim] // parts).reshape((-1,) + (1,) * (len(extent) - 1 - dim))
    return gain


def bell_draw(stream_key, dims, spread, bound, cuts=(), kind=jnp.bfloat16):
    array = spread * jax.random.normal(stream_key, dims, jnp.float32)
    if cuts:
        array = array * levels(stream_key, dims, cuts, -0.22, 0.18)
    return jnp.clip(array, -bound, bound).astype(kind)


def setup_inputs(seed: int = 0) -> dict:
    seeds = jax.random.split(jax.random.key(seed), 7)
    return {
        "residual": bell_draw(seeds[0], (PTS, PTS, PTS, ELEMS), 1.0, 6.0, ((3, 256),), jnp.float32),
        "eig_values": jnp.clip(jnp.exp(math.log(20.0) - 5.2983174 * jax.random.uniform(seeds[1], (3, EXT, ELEMS), jnp.float32) ** levels(seeds[1], (3, EXT, ELEMS), ((2, 256),), -0.2, 0.2)), 0.1, 20.0),
        "eig_vectors": bell_draw(seeds[2], (3, EXT, EXT, ELEMS), EXT ** -0.5, 1.75, ((3, 256),), jnp.float32),
        "corner_map": draw_corner_map(jax.random.fold_in(seeds[6], 71), 0),
        "stream_links": draw_stream_links(jax.random.fold_in(seeds[6], 71), 0),
        "coarse_inverse": draw_coarse_inverse(jax.random.fold_in(seeds[6], 71), 0),
    }


precise = lax.Precision.HIGHEST


def corner_table(points):
    spots = (2.0 * jnp.arange(points, dtype=jnp.float32) + 1.0) / points - 1.0
    return jnp.stack([(1.0 - spots) * 0.5, (1.0 + spots) * 0.5])


def along_direction(matrix, field, along, forward):
    count = matrix.shape[0]
    batch = field.shape[-1]
    total = None
    for index in range(count):
        piece = lax.index_in_dim(field, index, along, keepdims=True)
        if forward:
            coeff = matrix[index]
        else:
            coeff = matrix[:, index]
        shaped = [1, 1, 1, batch]
        shaped[along] = count
        term = coeff.reshape(tuple(shaped)) * piece
        total = term if total is None else total + term
    return total


def fast_solve(extended, eig_values, eig_vectors):
    moved = along_direction(eig_vectors[0], extended, 0, True)
    moved = along_direction(eig_vectors[1], moved, 1, True)
    moved = along_direction(eig_vectors[2], moved, 2, True)
    divisor = eig_values[0][:, None, None, :] + eig_values[1][None, :, None, :] + eig_values[2][None, None, :, :]
    moved = moved / divisor
    moved = along_direction(eig_vectors[0], moved, 0, False)
    moved = along_direction(eig_vectors[1], moved, 1, False)
    return along_direction(eig_vectors[2], moved, 2, False)


def to_grid(values_in):
    front = values_in.shape[:-1]
    leading = len(front)
    shaped = values_in.reshape(front + (SLABS, LAYERS, EX, EY, EZ))
    axes_order = tuple(range(leading)) + (leading, leading + 2, leading + 1, leading + 3, leading + 4)
    return jnp.transpose(shaped, axes_order).reshape(front + (SLABS * EX, LAYERS * EY, EZ))


def from_grid(values_in):
    front = values_in.shape[:-3]
    leading = len(front)
    shaped = values_in.reshape(front + (SLABS, EX, LAYERS, EY, EZ))
    axes_order = tuple(range(leading)) + (leading, leading + 2, leading + 1, leading + 3, leading + 4)
    return jnp.transpose(shaped, axes_order).reshape(front + (SLABS * LAYERS * EX * EY * EZ,))


def shift_up(planes, along):
    nothing = jnp.zeros_like(lax.slice_in_dim(planes, 0, 1, axis=along))
    kept = lax.slice_in_dim(planes, 0, planes.shape[along] - 1, axis=along)
    return jnp.concatenate([nothing, kept], axis=along)


def shift_down(planes, along):
    nothing = jnp.zeros_like(lax.slice_in_dim(planes, 0, 1, axis=along))
    kept = lax.slice_in_dim(planes, 1, planes.shape[along], axis=along)
    return jnp.concatenate([kept, nothing], axis=along)


def apply_inverse(paired):
    return jnp.dot(paired[0], paired[1], precision=precise)


def reference(residual, eig_values, eig_vectors, corner_map, stream_links, coarse_inverse):
    upstream = stream_links[0]
    downstream = stream_links[1]
    total = SLABS * LAYERS * EX * EY * EZ
    gridded = to_grid(residual)
    extended = jnp.zeros((EXT, EXT, EXT) + gridded.shape[3:], jnp.float32)
    extended = extended.at[1:-1, 1:-1, 1:-1].set(gridded)
    extended = extended.at[0, 1:-1, 1:-1].set(jnp.roll(gridded[PTS - 1], 1, axis=2))
    extended = extended.at[EXT - 1, 1:-1, 1:-1].set(jnp.roll(gridded[0], -1, axis=2))
    extended = extended.at[1:-1, 0, 1:-1].set(shift_up(gridded[:, PTS - 1], 3))
    extended = extended.at[1:-1, EXT - 1, 1:-1].set(shift_down(gridded[:, 0], 3))
    extended = extended.at[1:-1, 1:-1, 0].set(jnp.take(gridded[:, :, PTS - 1], upstream, axis=4))
    extended = extended.at[1:-1, 1:-1, EXT - 1].set(jnp.take(gridded[:, :, 0], downstream, axis=4))
    solved = fast_solve(extended.reshape(EXT, EXT, EXT, total),
                        to_grid(eig_values).reshape(3, EXT, total),
                        to_grid(eig_vectors).reshape(3, EXT, EXT, total)).reshape(extended.shape)
    solved_x0 = solved[0, 1:-1, 1:-1]
    solved_x1 = solved[EXT - 1, 1:-1, 1:-1]
    solved_y0 = solved[1:-1, 0, 1:-1]
    solved_y1 = solved[1:-1, EXT - 1, 1:-1]
    solved_z0 = solved[1:-1, 1:-1, 0]
    solved_z1 = solved[1:-1, 1:-1, EXT - 1]
    inner = solved[1:-1, 1:-1, 1:-1]
    inner = inner.at[0].add(jnp.roll(solved_x1, 1, axis=2))
    inner = inner.at[PTS - 1].add(jnp.roll(solved_x0, -1, axis=2))
    inner = inner.at[:, 0].add(shift_up(solved_y1, 3))
    inner = inner.at[:, PTS - 1].add(shift_down(solved_y0, 3))
    inner = inner.at[:, :, 0].add(jnp.take(solved_z1, upstream, axis=4))
    inner = inner.at[:, :, PTS - 1].add(jnp.take(solved_z0, downstream, axis=4))
    local_part = from_grid(inner)
    table = corner_table(PTS)
    corner_sums = jnp.einsum('at,bu,dv,tuve->abde', table, table, table, residual, precision=precise).reshape(8, total)
    slab_of = (jnp.arange(total, dtype=jnp.int32) // (LAYERS * EX * EY * EZ)).astype(jnp.int32)
    labels = corner_map + slab_of[None, :] * VERTS
    coarse_rhs = jax.ops.segment_sum(corner_sums.reshape(-1), labels.reshape(-1), num_segments=SLABS * VERTS)
    coarse_sol = lax.map(apply_inverse, (coarse_inverse, coarse_rhs.reshape(SLABS, VERTS)))
    at_corners = coarse_sol.reshape(-1)[labels].reshape(2, 2, 2, total)
    lifted = jnp.einsum('at,bu,dv,abde->tuve', table, table, table, at_corners, precision=precise)
    return local_part + lifted
```

```python
import functools

import jax
import jax.numpy as jnp
from jax import lax
from jax.experimental import pallas as pl
from jax.experimental.pallas import tpu as pltpu
from jax.sharding import PartitionSpec as P

PTS = 10
EXT = 12
EY = 8
EZ = 16
LANES = 128
SLAB = EXT * EXT
GROUP = 2 * EXT
POINT = tuple(range(1, PTS + 1)) + (0, EXT - 1)
LOW, HIGH = PTS, PTS + 1
precise = lax.Precision.HIGHEST
f32 = jnp.float32


def upper(index):
    return (2 * index + 1) / (2 * PTS)


def rows_of(shape):
    return lax.broadcasted_iota(jnp.int32, shape, 0)


def lanes_of(shape):
    return lax.broadcasted_iota(jnp.int32, shape, 1)


def turn(values, shift):
    return pltpu.roll(values, shift % LANES, 1)


def permute(values, index):
    return jnp.take_along_axis(values, jnp.broadcast_to(index, values.shape), axis=1)


def divider(rows, top):
    for shift in range(12, 26):
        factor = -(-(1 << shift) // rows)
        if top * factor < 1 << 31 and all((v * factor) >> shift == v // rows for v in range(top)):
            return factor, shift
    raise ValueError("no divider")


def contract(count, groups, first, load, coeff, store):
    def body(group, carry):
        pieces = load(group)
        for o in range(EXT):
            total = None
            for i in range(count):
                term = coeff(o, i) * pieces[i]
                total = term if total is None else total + term
            store(group, o, total)
        return carry

    lax.fori_loop(first, groups, body, 0)


def kernel(
    spans, walls, verts,
    res_in, val_in, vec_in, map_in, link_in, inv_in, out,
    field, faces, ping, pong, solved, vec, val, cmap, links, inv,
    acc, csum, xown, xall, yown, yall, pack_out, pack_in, face_in,
    local_sem, out_sem, span_send, span_recv, wall_send, wall_recv, x_send, x_recv, y_send, y_recv,
):
    s = lax.axis_index("span")
    w = lax.axis_index("wall")
    rows = verts // walls
    tiles = verts // LANES
    rest = verts - tiles * LANES
    inner = pl.ds(0, PTS)

    load_field = pltpu.make_async_copy(res_in, field.at[inner, inner, inner, :], local_sem.at[0])
    load_map = pltpu.make_async_copy(map_in, cmap, local_sem.at[1])
    load_links = pltpu.make_async_copy(link_in, links, local_sem.at[2])
    load_vec = pltpu.make_async_copy(vec_in, vec, local_sem.at[3])
    load_val = pltpu.make_async_copy(val_in, val, local_sem.at[4])
    load_inv = pltpu.make_async_copy(inv_in.at[0], inv, local_sem.at[5])
    for copy in (load_field, load_map, load_links, load_vec, load_val, load_inv):
        copy.start()

    barrier = pltpu.get_barrier_semaphore()
    for k in range(1, walls):
        pl.semaphore_signal(barrier, inc=1, device_id={"wall": lax.rem(w + k, walls)})
    above = lax.rem(s + 1, spans)
    below = lax.rem(s + spans - 1, spans)
    for peer in (above, below):
        pl.semaphore_signal(barrier, inc=1, device_id={"span": peer})
    pl.semaphore_wait(barrier, walls + 1)

    def remote(src, dst, send, recv, axis, peer):
        return pltpu.make_async_remote_copy(
            src_ref=src, dst_ref=dst, send_sem=send, recv_sem=recv, device_id={axis: peer}
        )

    span_first = [
        remote(res_in.at[PTS - 1], faces.at[0, inner, inner, :], span_send.at[0], span_recv.at[0], "span", above),
        remote(res_in.at[0], faces.at[1, inner, inner, :], span_send.at[1], span_recv.at[1], "span", below),
    ]
    for copy in span_first:
        copy.start()

    def wall_copies(turn_index):
        base = 2 * turn_index
        up = remote(pack_out.at[base], pack_in.at[base], wall_send.at[base], wall_recv.at[base],
                    "wall", lax.rem(w + 1, walls))
        down = remote(pack_out.at[base + 1], pack_in.at[base + 1], wall_send.at[base + 1], wall_recv.at[base + 1],
                      "wall", lax.rem(w + walls - 1, walls))
        return up, down

    has_up = w < walls - 1
    has_down = w > 0

    def send_walls(turn_index):
        up, down = wall_copies(turn_index)
        pl.when(has_up)(up.start)
        pl.when(has_down)(down.start)

    def receive_walls(turn_index):
        up, down = wall_copies(turn_index)
        pl.when(has_down)(up.wait_recv)
        pl.when(has_up)(down.wait_recv)

    def finish_walls(turn_index):
        up, down = wall_copies(turn_index)
        pl.when(has_up)(up.wait_send)
        pl.when(has_down)(down.wait_send)

    lane = lanes_of((8, LANES))
    slot_of = lane // EZ

    def pack(source, layer, lane_from, dest):
        parts = [None] * 3
        for t in range(PTS):
            for half in range(2):
                slot = 2 * t + half
                piece = source[t, layer, pl.ds(8 * half, 8), :]
                place = slot % 8
                moved = turn(piece, EZ * place - lane_from)
                held = parts[slot // 8]
                parts[slot // 8] = moved if held is None else jnp.where(slot_of == place, moved, held)
        for index, part in enumerate(parts):
            pack_out[dest, pl.ds(8 * index, 8), :] = part

    def unpack(buffer, t, half, lane_to):
        slot = 2 * t + half
        part = pack_in[buffer, pl.ds(8 * (slot // 8), 8), :]
        return turn(part, lane_to - EZ * (slot % 8))

    @pl.when(jnp.logical_not(has_down))
    def _():
        for turn_index in range(2):
            pack_in[2 * turn_index] = jnp.zeros(pack_in.shape[1:], f32)

    @pl.when(jnp.logical_not(has_up))
    def _():
        for turn_index in range(2):
            pack_in[2 * turn_index + 1] = jnp.zeros(pack_in.shape[1:], f32)

    blank = jnp.zeros((16 - PTS, LANES), f32)
    for t in range(PTS):
        field[t, 0, pl.ds(PTS, 16 - PTS), :] = blank
        field[t, PTS - 1, pl.ds(PTS, 16 - PTS), :] = blank
    for side in range(2):
        for u in (LOW, HIGH):
            faces[side, u] = jnp.zeros((16, LANES), f32)
    csum[...] = jnp.zeros(csum.shape, f32)
    acc[...] = jnp.zeros(acc.shape, f32)

    load_links.wait()
    lane_row = lanes_of((8, LANES))
    place = lane_row % EZ
    up_slot = jnp.zeros((8, LANES), jnp.int32)
    down_slot = jnp.zeros((8, LANES), jnp.int32)
    for q in range(EZ):
        up_slot = jnp.where(place == q, links[0, q], up_slot)
        down_slot = jnp.where(place == q, links[1, q], down_slot)
    line = lane_row - place
    upstream8 = line + up_slot
    downstream8 = line + down_slot
    upstream = jnp.concatenate([upstream8] * 3, axis=0)
    downstream = jnp.concatenate([downstream8] * 3, axis=0)

    load_field.wait()
    pack(field, PTS - 1, LANES - EZ, 0)
    pack(field, 0, 0, 1)
    send_walls(0)

    def corner_body(u, sums):
        total = None
        weighted = None
        for t in range(PTS):
            piece = field[t, u, inner, :]
            term = piece * upper(t)
            total = piece if total is None else total + piece
            weighted = term if weighted is None else weighted + term
        low = total - weighted
        share = (2.0 * u.astype(f32) + 1.0) / (2 * PTS)
        low_up = low * share
        high_up = weighted * share
        return (sums[0] + (low - low_up), sums[1] + low_up,
                sums[2] + (weighted - high_up), sums[3] + high_up)

    nothing = jnp.zeros((PTS, LANES), f32)
    sums = lax.fori_loop(0, PTS, corner_body, (nothing,) * 4)
    share_v = (2.0 * rows_of((PTS, LANES)).astype(f32) + 1.0) / (2 * PTS)
    for ab in range(4):
        upper_part = sums[ab] * share_v
        csum[0, pl.ds(ab, 1), :] = jnp.sum(sums[ab] - upper_part, axis=0, keepdims=True)
        csum[1, pl.ds(ab, 1), :] = jnp.sum(upper_part, axis=0, keepdims=True)
    lines = csum[0] + permute(csum[1], upstream8)
    moved_up = jnp.where(lane >= EZ, turn(lines, EZ), 0.0)
    moved_down = turn(lines, -EZ)
    lane1 = lanes_of((1, LANES))
    last_line = lane1 >= LANES - EZ
    second_line = lane1 >= LANES - 2 * EZ
    values = jnp.concatenate([
        lines[0:1] + moved_up[1:2],
        lines[2:3] + moved_up[3:4],
        jnp.where(last_line, lines[1:2], jnp.where(second_line, moved_down[3:4], 0.0)),
    ], axis=1)

    load_map.wait()
    moved_map = turn(cmap[...], -EZ)
    ids = jnp.concatenate([
        cmap[0:1, :],
        cmap[4:5, :],
        jnp.where(last_line, cmap[2:3, :], jnp.where(second_line, moved_map[6:7], -1)),
    ], axis=1)
    width = 3 * LANES
    held = xown.shape[0]
    spread = jnp.where(rows_of((held, width)) == (ids >> 7), values, 0.0)
    onehot = (rows_of((LANES, width)) == (ids & (LANES - 1))).astype(f32)
    xown[...] = lax.dot_general(
        spread, onehot, (((1,), (1,)), ((), ())), precision=precise, preferred_element_type=f32
    )

    def x_copy(k):
        return remote(xown, xall.at[k], x_send.at[k], x_recv.at[k], "wall", lax.rem(w + k, walls))

    for k in range(1, walls):
        x_copy(k).start()

    receive_walls(0)
    first_line = lane < EZ
    end_line = lane >= LANES - EZ
    for t in range(PTS):
        for half in range(2):
            span_rows = pl.ds(8 * half, 8)
            low = turn(field[t, PTS - 1, span_rows, :], EZ)
            field[t, LOW, span_rows, :] = jnp.where(first_line, unpack(0, t, half, 0), low)
            high = turn(field[t, 0, span_rows, :], -EZ)
            field[t, HIGH, span_rows, :] = jnp.where(end_line, unpack(1, t, half, LANES - EZ), high)

    def vector(direction, point, mode):
        return jnp.broadcast_to(vec[direction, point, pl.ds(mode, 1), :], (GROUP, LANES))

    def strided(ref):
        return lambda g: [ref[pl.ds(g * (GROUP * EXT) + i, GROUP, stride=EXT), :] for i in range(EXT)]

    def dense(ref):
        def put(g, o, total):
            ref[pl.ds(pl.multiple_of(o * SLAB + g * GROUP, 8), GROUP), :] = total
        return put

    load_vec.wait()
    load_val.wait()
    flat_field = field.reshape(PTS * EXT * 16, LANES)
    flat_faces = faces.reshape(2 * EXT * 16, LANES)
    inside = (rows_of((GROUP, LANES)) % EXT) < PTS

    def load_first(g):
        pieces = [flat_field[pl.ds(g * (GROUP * 16) + v, GROUP, stride=16), :] for v in range(PTS)]
        pieces.append(jnp.where(inside, permute(pieces[PTS - 1], upstream), 0.0))
        pieces.append(jnp.where(inside, permute(pieces[0], downstream), 0.0))
        return pieces

    def load_faces(g):
        return [flat_faces[pl.ds(v, GROUP, stride=16), :] for v in range(PTS)]

    forward = lambda d: lambda o, i: vector(d, POINT[i], o)
    backward = lambda d: lambda o, i: vector(d, POINT[o], i)
    contract(EXT, PTS // 2, 0, load_first, forward(2), dense(ping))
    for copy in span_first:
        copy.wait_recv()
    contract(PTS, EXT // 2, PTS // 2, load_faces, forward(2), dense(ping))
    contract(EXT, EXT // 2, 0, strided(ping), forward(1), dense(pong))

    second_half = rows_of((GROUP, LANES)) >= EXT
    third = jnp.concatenate([val[2], val[2]], axis=0)

    def scaled(ref):
        put = dense(ref)

        def divide(g, o, total):
            firsts = jnp.broadcast_to(val[1, pl.ds(2 * g, 1), :], (GROUP, LANES))
            seconds = jnp.broadcast_to(val[1, pl.ds(2 * g + 1, 1), :], (GROUP, LANES))
            both = jnp.where(second_half, seconds, firsts) + third
            put(g, o, total / (jnp.broadcast_to(val[0, pl.ds(o, 1), :], (GROUP, LANES)) + both))
        return divide

    contract(EXT, EXT // 2, 0, strided(pong), forward(0), scaled(ping))

    load_inv.wait()
    for k in range(1, walls):
        x_copy(k).wait_recv()
    total_x = xown[...]
    for k in range(1, walls):
        total_x = total_x + xall[k]
    xall[0] = total_x

    def times(start, count):
        total = None
        for c in range(tiles):
            term = inv[pl.ds(start, count), pl.ds(c * LANES, LANES)] * xall[0, pl.ds(c, 1), :]
            total = term if total is None else total + term
        acc[0, pl.ds(start, count), :] = total
        if rest:
            tail = inv[pl.ds(start, count), pl.ds(tiles * LANES, rest)] * xall[0, pl.ds(tiles, 1), pl.ds(0, rest)]
            acc[1, pl.ds(start, count), pl.ds(0, rest)] = tail

    chunk = 32
    whole = rows // chunk

    def times_body(r, carry):
        times(pl.multiple_of(r * chunk, chunk), chunk)
        return carry

    lax.fori_loop(0, whole, times_body, 0)
    if rows - whole * chunk:
        times(whole * chunk, rows - whole * chunk)
    ones = jnp.ones((8, LANES), f32)
    own = lax.dot_general(
        ones, acc[0] + acc[1], (((1,), (1,)), ((), ())), precision=precise, preferred_element_type=f32
    )
    row8 = rows_of((8, LANES))
    tile = own[:, 0:LANES]
    for part in range(1, acc.shape[1] // LANES):
        tile = jnp.where(row8 == part, own[:, part * LANES : (part + 1) * LANES], tile)
    yown[...] = tile
    yall[w] = tile

    def y_copy(k):
        return remote(yown, yall.at[w], y_send.at[k], y_recv.at[k], "wall", lax.rem(w + k, walls))

    def y_arrival(k):
        sender = lax.rem(w + walls - k, walls)
        return remote(yown, yall.at[sender], y_send.at[k], y_recv.at[k], "wall", sender)

    for k in range(1, walls):
        y_copy(k).start()

    contract(EXT, EXT // 2, 0, strided(ping), backward(2), dense(pong))
    contract(EXT, EXT // 2, 0, strided(pong), backward(1), dense(ping))

    def place_points(g, o, total):
        solved[o, 2 * g, pl.ds(0, EXT), :] = total[0:EXT]
        solved[o, 2 * g + 1, pl.ds(0, EXT), :] = total[EXT:GROUP]

    contract(EXT, EXT // 2, 0, strided(ping), backward(0), place_points)

    span_second = [
        remote(solved.at[HIGH, inner, inner, :], face_in.at[0, :, inner, :], span_send.at[2], span_recv.at[2], "span", above),
        remote(solved.at[LOW, inner, inner, :], face_in.at[1, :, inner, :], span_send.at[3], span_recv.at[3], "span", below),
    ]
    for copy in span_second:
        copy.start()
    blank4 = jnp.zeros((16 - EXT, LANES), f32)
    for t in range(PTS):
        solved[t, LOW, pl.ds(EXT, 16 - EXT), :] = blank4
        solved[t, HIGH, pl.ds(EXT, 16 - EXT), :] = blank4
    pack(solved, HIGH, LANES - EZ, 2)
    pack(solved, LOW, 0, 3)
    send_walls(1)

    flat_solved = solved.reshape(EXT * EXT * 16, LANES)

    def stream_body(g, carry):
        def at(v):
            return pl.ds(g * (GROUP * 16) + v, GROUP, stride=16)
        low = jnp.where(inside, permute(flat_solved[at(HIGH), :], upstream), 0.0)
        high = jnp.where(inside, permute(flat_solved[at(LOW), :], downstream), 0.0)
        flat_solved[at(0), :] = flat_solved[at(0), :] + low
        flat_solved[at(PTS - 1), :] = flat_solved[at(PTS - 1), :] + high
        return carry

    lax.fori_loop(0, PTS // 2, stream_body, 0)

    for k in range(1, walls):
        y_arrival(k).wait_recv()
    factor, shift = divider(rows, verts)
    known = jnp.maximum(ids, 0)
    owner = (known * factor) >> shift
    local = known - owner * rows
    wanted = owner * 8 + (local >> 7)
    column = (rows_of((LANES, width)) == (local & (LANES - 1))).astype(f32)
    table = jnp.dot(yall[...].reshape(8 * walls, LANES), column, precision=precise, preferred_element_type=f32)
    found = jnp.sum(jnp.where(rows_of((8 * walls, width)) == wanted, table, 0.0), axis=0, keepdims=True)
    tops = found[:, 2 * LANES :]
    top = (tops, turn(tops, EZ))
    for a in range(2):
        base = found[:, a * LANES : (a + 1) * LANES]
        csum[0, pl.ds(2 * a, 1), :] = base
        csum[0, pl.ds(2 * a + 1, 1), :] = jnp.where(last_line, top[a], turn(base, -EZ))
    near = csum[0]
    far = permute(near, downstream8)
    across = []
    for ab in range(4):
        begin = jnp.broadcast_to(near[ab : ab + 1], (PTS, LANES))
        end = jnp.broadcast_to(far[ab : ab + 1], (PTS, LANES))
        across.append(begin + (end - begin) * share_v)

    def lift_body(u, carry):
        share = (2.0 * u.astype(f32) + 1.0) / (2 * PTS)
        low = across[0] + (across[1] - across[0]) * share
        high = across[2] + (across[3] - across[2]) * share
        step = high - low
        for t in range(PTS):
            solved[t, u, inner, :] = solved[t, u, inner, :] + (low + step * upper(t))
        return carry

    lax.fori_loop(0, PTS, lift_body, 0)

    receive_walls(1)
    for t in range(PTS):
        for half in range(2):
            span_rows = pl.ds(8 * half, 8)
            low = jnp.where(first_line, unpack(2, t, half, 0), turn(solved[t, HIGH, span_rows, :], EZ))
            high = jnp.where(end_line, unpack(3, t, half, LANES - EZ), turn(solved[t, LOW, span_rows, :], -EZ))
            count = 8 if half == 0 else PTS - 8
            kept = pl.ds(8 * half, count)
            solved[t, 0, kept, :] = solved[t, 0, kept, :] + low[0:count]
            solved[t, PTS - 1, kept, :] = solved[t, PTS - 1, kept, :] + high[0:count]

    def out_copy(t):
        return pltpu.make_async_copy(solved.at[t, inner, inner, :], out.at[t], out_sem.at[t])

    for t in range(1, PTS - 1):
        out_copy(t).start()
    for side, layer in ((0, 0), (1, PTS - 1)):
        span_second[side].wait_recv()

        def span_body(u, carry):
            solved[layer, u, inner, :] = solved[layer, u, inner, :] + face_in[side, u, inner, :]
            return carry

        lax.fori_loop(0, PTS, span_body, 0)
        out_copy(layer).start()

    for copy in span_first + span_second:
        copy.wait_send()
    finish_walls(0)
    finish_walls(1)
    for k in range(1, walls):
        x_copy(k).wait_send()
        y_copy(k).wait_send()
    for t in range(PTS):
        out_copy(t).wait()


def solution(mesh):
    spans, walls = mesh.shape["span"], mesh.shape["wall"]

    def per_device(residual, eig_values, eig_vectors, corner_map, stream_links, coarse_inverse):
        rows, verts = coarse_inverse.shape[1:]
        held = -(-verts // LANES)
        held = -(-held // 8) * 8
        padded = -(-rows // LANES) * LANES
        vmem = lambda *shape: pltpu.VMEM(shape, f32)
        dma = lambda count: pltpu.SemaphoreType.DMA((count,))
        return pl.pallas_call(
            functools.partial(kernel, spans, walls, verts),
            out_shape=jax.ShapeDtypeStruct(residual.shape, f32),
            in_specs=[pl.BlockSpec(memory_space=pl.ANY)] * 6,
            out_specs=pl.BlockSpec(memory_space=pl.ANY),
            scratch_shapes=[
                vmem(PTS, EXT, 16, LANES),
                vmem(2, EXT, 16, LANES),
                vmem(EXT * SLAB, LANES),
                vmem(EXT * SLAB, LANES),
                vmem(EXT, EXT, 16, LANES),
                vmem(*eig_vectors.shape),
                vmem(*eig_values.shape),
                pltpu.VMEM(corner_map.shape, jnp.int32),
                pltpu.SMEM(stream_links.shape, jnp.int32),
                vmem(rows, verts),
                vmem(2, padded, LANES),
                vmem(2, 8, LANES),
                vmem(held, LANES),
                vmem(walls, held, LANES),
                vmem(8, LANES),
                vmem(walls, 8, LANES),
                vmem(4, 24, LANES),
                vmem(4, 24, LANES),
                vmem(2, PTS, 16, LANES),
                dma(6), dma(PTS), dma(4), dma(4), dma(4), dma(4),
                dma(walls), dma(walls), dma(walls), dma(walls),
            ],
            compiler_params=pltpu.CompilerParams(
                collective_id=0, has_side_effects=True, vmem_limit_bytes=40 * 2**20
            ),
        )(residual, eig_values, eig_vectors, corner_map, stream_links, coarse_inverse)

    return jax.shard_map(
        per_device,
        mesh=mesh,
        in_specs=(
            P(None, None, None, ("span", "wall")),
            P(None, None, ("span", "wall")),
            P(None, None, None, ("span", "wall")),
            P(None, ("span", "wall")),
            P(),
            P("span", "wall", None),
        ),
        out_specs=P(None, None, None, ("span", "wall")),
        check_vma=False,
    )
```

```python
import functools

import jax
import jax.numpy as jnp
from jax import lax
from jax.experimental import pallas as pl
from jax.experimental.pallas import tpu as pltpu
from jax.sharding import PartitionSpec as P

PTS = 10
EXT = 12
EY = 8
EZ = 16
LANES = 128
SLAB = EXT * EXT
GROUP = 2 * EXT
POINT = tuple(range(1, PTS + 1)) + (0, EXT - 1)
LOW, HIGH = PTS, PTS + 1
precise = lax.Precision.HIGHEST
f32 = jnp.float32


def upper(index):
    return (2 * index + 1) / (2 * PTS)


def rows_of(shape):
    return lax.broadcasted_iota(jnp.int32, shape, 0)


def lanes_of(shape):
    return lax.broadcasted_iota(jnp.int32, shape, 1)


def turn(values, shift):
    return pltpu.roll(values, shift % LANES, 1)


def permute(values, index):
    return jnp.take_along_axis(values, jnp.broadcast_to(index, values.shape), axis=1)


def exact(values, picks, dims):
    picks = picks.astype(jnp.bfloat16)
    total = None
    for _ in range(3):
        piece = values.astype(jnp.bfloat16)
        values = values - piece.astype(f32)
        term = lax.dot_general(piece, picks, (dims, ((), ())), preferred_element_type=f32)
        total = term if total is None else total + term
    return total


def divider(rows, top):
    for shift in range(12, 26):
        factor = -(-(1 << shift) // rows)
        if top * factor < 1 << 31 and all((v * factor) >> shift == v // rows for v in range(top)):
            return factor, shift
    raise ValueError("no divider")


def contract(count, groups, first, load, coeff, store, outputs=range(EXT)):
    def body(group, carry):
        pieces = load(group)
        for o in outputs:
            total = None
            for i in range(count):
                term = coeff(o, i) * pieces[i]
                total = term if total is None else total + term
            store(group, o, total)
        return carry

    lax.fori_loop(first, groups, body, 0)


def kernel(
    spans, walls, verts,
    res_in, val_in, vec_in, map_in, link_in, inv_in, out, corners_out,
    field, faces, wall_face, ping, pong, face_ping, face_pong, wall_ping, wall_pong, part, mixed, solved,
    vec, val, cmap, links, inv, acc, csum, xown, xall, yown, yall, pack_out, pack_in, face_in,
    local_sem, out_sem, span_send, span_recv, wall_send, wall_recv, x_send, x_recv, y_send, y_recv, meet,
):
    s = lax.axis_index("span")
    w = lax.axis_index("wall")
    rows = verts // walls
    tiles = verts // LANES
    rest = verts - tiles * LANES
    inner = pl.ds(0, PTS)

    load_field = pltpu.make_async_copy(res_in, field.at[inner, inner, inner, :], local_sem.at[0])
    load_map = pltpu.make_async_copy(map_in, cmap, local_sem.at[1])
    load_links = pltpu.make_async_copy(link_in, links, local_sem.at[2])
    load_vec = pltpu.make_async_copy(vec_in, vec, local_sem.at[3])
    load_val = pltpu.make_async_copy(val_in, val, local_sem.at[4])
    load_inv = pltpu.make_async_copy(inv_in.at[:, 0, :], inv, local_sem.at[5])
    for copy in (load_links, load_map, load_field, load_vec, load_val):
        copy.start()

    across_count = 4 if walls == 16 else 1
    along_count = walls // across_count
    row, column = lax.div(w, across_count), lax.rem(w, across_count)

    def partner(k, sign):
        down, right = k // across_count, k % across_count
        if sign < 0:
            down, right = along_count - down, across_count - right
        return lax.rem(row + down, along_count) * across_count + lax.rem(column + right, across_count)

    def hops(k):
        down, right = k // across_count, k % across_count
        return min(down, along_count - down) + min(right, across_count - right)

    partners = sorted(range(1, walls), key=lambda k: -hops(k))

    above = lax.rem(s + 1, spans)
    below = lax.rem(s + spans - 1, spans)
    even = lax.rem(s, 2) == 0
    hears_above = jnp.logical_or(even, s == spans - 1)
    hears_below = jnp.logical_and(even, s > 0)
    speaks_above = jnp.logical_not(hears_above)
    speaks_below = jnp.logical_not(hears_below)
    barrier = pltpu.get_barrier_semaphore()
    for k in partners:
        pl.semaphore_signal(barrier, inc=1, device_id={"wall": partner(k, 1)})

    @pl.when(speaks_above)
    def _():
        pl.semaphore_signal(barrier, inc=1, device_id={"span": above})

    @pl.when(speaks_below)
    def _():
        pl.semaphore_signal(barrier, inc=1, device_id={"span": below})

    def remote(src, dst, send, recv, axis, peer):
        return pltpu.make_async_remote_copy(
            src_ref=src, dst_ref=dst, send_sem=send, recv_sem=recv, device_id={axis: peer}
        )

    span_first = [
        remote(res_in.at[PTS - 1], faces.at[0, inner, inner, :], span_send.at[0], span_recv.at[0], "span", above),
        remote(res_in.at[0], faces.at[1, inner, inner, :], span_send.at[1], span_recv.at[1], "span", below),
    ]
    def wall_copies(turn_index):
        base = 2 * turn_index
        up = remote(pack_out.at[base], pack_in.at[base], wall_send.at[base], wall_recv.at[base],
                    "wall", lax.rem(w + 1, walls))
        down = remote(pack_out.at[base + 1], pack_in.at[base + 1], wall_send.at[base + 1], wall_recv.at[base + 1],
                      "wall", lax.rem(w + walls - 1, walls))
        return up, down

    has_up = w < walls - 1
    has_down = w > 0

    def send_walls(turn_index):
        up, down = wall_copies(turn_index)
        pl.when(has_up)(up.start)
        pl.when(has_down)(down.start)

    def receive_walls(turn_index):
        up, down = wall_copies(turn_index)
        pl.when(has_down)(up.wait_recv)
        pl.when(has_up)(down.wait_recv)

    def finish_walls(turn_index):
        up, down = wall_copies(turn_index)
        pl.when(has_up)(up.wait_send)
        pl.when(has_down)(down.wait_send)

    lane = lanes_of((8, LANES))
    slot_of = lane // EZ

    def pack(source, layer, lane_from, dest):
        parts = [None] * 3
        for t in range(PTS):
            for half in range(2):
                slot = 2 * t + half
                piece = source[t, layer, pl.ds(8 * half, 8), :]
                place = slot % 8
                moved = turn(piece, EZ * place - lane_from)
                held = parts[slot // 8]
                parts[slot // 8] = moved if held is None else jnp.where(slot_of == place, moved, held)
        for index, part in enumerate(parts):
            pack_out[dest, pl.ds(8 * index, 8), :] = part

    def unpack(buffer, t, half, lane_to):
        slot = 2 * t + half
        part = pack_in[buffer, pl.ds(8 * (slot // 8), 8), :]
        return turn(part, lane_to - EZ * (slot % 8))

    @pl.when(jnp.logical_not(has_down))
    def _():
        for turn_index in range(2):
            pack_in[2 * turn_index] = jnp.zeros(pack_in.shape[1:], f32)

    @pl.when(jnp.logical_not(has_up))
    def _():
        for turn_index in range(2):
            pack_in[2 * turn_index + 1] = jnp.zeros(pack_in.shape[1:], f32)

    blank = jnp.zeros((16 - PTS, LANES), f32)
    for t in range(PTS):
        field[t, 0, pl.ds(PTS, 16 - PTS), :] = blank
        field[t, PTS - 1, pl.ds(PTS, 16 - PTS), :] = blank
    for side in range(2):
        for u in (LOW, HIGH):
            faces[side, u] = jnp.zeros((16, LANES), f32)
    csum[...] = jnp.zeros(csum.shape, f32)
    acc[...] = jnp.zeros(acc.shape, f32)

    load_links.wait()
    lane_row = lanes_of((8, LANES))
    place = lane_row % EZ
    up_slot = jnp.zeros((8, LANES), jnp.int32)
    down_slot = jnp.zeros((8, LANES), jnp.int32)
    for q in range(EZ):
        up_slot = jnp.where(place == q, links[0, q], up_slot)
        down_slot = jnp.where(place == q, links[1, q], down_slot)
    line = lane_row - place
    upstream8 = line + up_slot
    downstream8 = line + down_slot
    upstream = jnp.concatenate([upstream8] * 3, axis=0)
    downstream = jnp.concatenate([downstream8] * 3, axis=0)

    load_field.wait()
    pack(field, PTS - 1, LANES - EZ, 0)
    pack(field, 0, 0, 1)
    greeted = walls - 1 + hears_above.astype(jnp.int32) + hears_below.astype(jnp.int32)
    pl.semaphore_wait(barrier, greeted)
    send_walls(0)

    @pl.when(hears_above)
    def _():
        pl.semaphore_signal(meet.at[1], inc=1, device_id={"span": above})
        span_first[0].start()

    @pl.when(hears_below)
    def _():
        pl.semaphore_signal(meet.at[0], inc=1, device_id={"span": below})
        span_first[1].start()

    def corner_body(u, sums):
        total = None
        weighted = None
        for t in range(PTS):
            piece = field[t, u, inner, :]
            term = piece * upper(t)
            total = piece if total is None else total + piece
            weighted = term if weighted is None else weighted + term
        low = total - weighted
        share = (2.0 * u.astype(f32) + 1.0) / (2 * PTS)
        low_up = low * share
        high_up = weighted * share
        return (sums[0] + (low - low_up), sums[1] + low_up,
                sums[2] + (weighted - high_up), sums[3] + high_up)

    nothing = jnp.zeros((PTS, LANES), f32)
    sums = lax.fori_loop(0, PTS, corner_body, (nothing,) * 4)
    share_v = (2.0 * rows_of((PTS, LANES)).astype(f32) + 1.0) / (2 * PTS)
    for ab in range(4):
        upper_part = sums[ab] * share_v
        csum[0, pl.ds(ab, 1), :] = jnp.sum(sums[ab] - upper_part, axis=0, keepdims=True)
        csum[1, pl.ds(ab, 1), :] = jnp.sum(upper_part, axis=0, keepdims=True)
    lines = csum[0] + permute(csum[1], upstream8)
    moved_up = jnp.where(lane >= EZ, turn(lines, EZ), 0.0)
    moved_down = turn(lines, -EZ)
    lane1 = lanes_of((1, LANES))
    last_line = lane1 >= LANES - EZ
    second_line = lane1 >= LANES - 2 * EZ
    values = jnp.concatenate([
        lines[0:1] + moved_up[1:2],
        lines[2:3] + moved_up[3:4],
        jnp.where(last_line, lines[1:2], jnp.where(second_line, moved_down[3:4], 0.0)),
    ], axis=1)

    load_map.wait()
    moved_map = turn(cmap[...], -EZ)
    ids = jnp.concatenate([
        cmap[0:1, :],
        cmap[4:5, :],
        jnp.where(last_line, cmap[2:3, :], jnp.where(second_line, moved_map[6:7], -1)),
    ], axis=1)
    width = 3 * LANES
    held = xown.shape[0]
    used = pl.ds(0, tiles + (1 if rest else 0))
    spread = jnp.where(rows_of((held, width)) == (ids >> 7), values, 0.0)
    onehot = (rows_of((LANES, width)) == (ids & (LANES - 1))).astype(f32)
    xown[...] = exact(spread, onehot, ((1,), (1,)))

    def x_copy(k):
        return remote(xown.at[used], xall.at[k, used], x_send.at[k], x_recv.at[k], "wall", partner(k, 1))

    for k in partners:
        x_copy(k).start()

    load_inv.start()

    first_line = lane < EZ
    end_line = lane >= LANES - EZ

    def wall_body(t, carry):
        for half in range(2):
            span_rows = pl.ds(8 * half, 8)
            low = turn(field[t, PTS - 1, span_rows, :], EZ)
            field[t, LOW, span_rows, :] = jnp.where(first_line, 0.0, low)
            high = turn(field[t, 0, span_rows, :], -EZ)
            field[t, HIGH, span_rows, :] = jnp.where(end_line, 0.0, high)
        return carry

    lax.fori_loop(0, PTS, wall_body, 0)

    @pl.when(speaks_above)
    def _():
        pl.semaphore_wait(meet.at[0], 1)
        span_first[0].start()

    @pl.when(jnp.logical_not(even))
    def _():
        pl.semaphore_wait(meet.at[1], 1)
        span_first[1].start()

    def vector(direction, point, mode):
        return jnp.broadcast_to(vec[direction, point, pl.ds(mode, 1), :], (GROUP, LANES))

    def strided(ref, count=EXT):
        return lambda g: [ref[pl.ds(g * (GROUP * count) + i, GROUP, stride=count), :] for i in range(count)]

    def dense(ref, length=SLAB):
        def put(g, o, total):
            ref[pl.ds(pl.multiple_of(o * length + g * GROUP, 8), GROUP), :] = total
        return put

    load_vec.wait()
    load_val.wait()
    flat_field = field.reshape(PTS * EXT * 16, LANES)
    flat_faces = faces.reshape(2 * EXT * 16, LANES)
    inside = (rows_of((GROUP, LANES)) % EXT) < PTS

    def load_first(g):
        pieces = [flat_field[pl.ds(g * (GROUP * 16) + v, GROUP, stride=16), :] for v in range(PTS)]
        pieces.append(jnp.where(inside, permute(pieces[PTS - 1], upstream), 0.0))
        pieces.append(jnp.where(inside, permute(pieces[0], downstream), 0.0))
        return pieces

    def load_faces(g):
        return [flat_faces[pl.ds(v, GROUP, stride=16), :] for v in range(PTS)]

    forward = lambda d: lambda o, i: vector(d, POINT[i], o)
    backward = lambda d: lambda o, i: vector(d, POINT[o], i)
    short = EXT * PTS
    contract(EXT, PTS // 2, 0, load_first, forward(2), dense(ping, short))
    contract(EXT, PTS // 2, 0, strided(ping), forward(1), dense(pong, short))
    contract(PTS, EXT // 2, 0, strided(pong, PTS), forward(0), dense(part))

    @pl.when(s == 0)
    def _():
        pl.semaphore_wait(meet.at[1], 1)
        span_first[1].start()

    def y_copy(k):
        return remote(yown, yall.at[w], y_send.at[k], y_recv.at[k], "wall", partner(k, 1))

    def y_arrival(k):
        sender = partner(k, -1)
        return remote(yown, yall.at[sender], y_send.at[k], y_recv.at[k], "wall", sender)

    def coarse_solve():
        load_inv.wait()
        for k in range(1, walls):
            x_copy(k).wait_recv()
        total_x = xown[...]
        for k in range(1, walls):
            total_x = total_x + xall[k]
        xall[0] = total_x

        def times(start, count):
            total = None
            for c in range(tiles):
                term = inv[pl.ds(start, count), pl.ds(c * LANES, LANES)] * xall[0, pl.ds(c, 1), :]
                total = term if total is None else total + term
            acc[0, pl.ds(start, count), :] = total
            if rest:
                tail = inv[pl.ds(start, count), pl.ds(tiles * LANES, rest)] * xall[0, pl.ds(tiles, 1), pl.ds(0, rest)]
                acc[1, pl.ds(start, count), pl.ds(0, rest)] = tail

        chunk = 32
        whole = rows // chunk

        def times_body(r, carry):
            times(pl.multiple_of(r * chunk, chunk), chunk)
            return carry

        lax.fori_loop(0, whole, times_body, 0)
        if rows - whole * chunk:
            times(whole * chunk, rows - whole * chunk)
        ones = jnp.ones((8, LANES), f32)
        own = lax.dot_general(
            ones, acc[0] + acc[1], (((1,), (1,)), ((), ())), precision=precise, preferred_element_type=f32
        )
        row8 = rows_of((8, LANES))
        tile = own[:, 0:LANES]
        for part in range(1, acc.shape[1] // LANES):
            tile = jnp.where(row8 == part, own[:, part * LANES : (part + 1) * LANES], tile)
        yown[...] = tile
        yall[w] = tile

        for k in partners:
            y_copy(k).start()

    pl.when(s == 0)(coarse_solve)

    receive_walls(0)
    for t in range(PTS):
        for half in range(2):
            kept = jnp.where(end_line, unpack(1, t, half, LANES - EZ), 0.0)
            wall_face[t, pl.ds(8 * half, 8), :] = jnp.where(first_line, unpack(0, t, half, 0), kept)
    flat_wall = wall_face.reshape(PTS * 16, LANES)
    pieces = [flat_wall[pl.ds(v, PTS, stride=16), :] for v in range(PTS)]
    for o in range(EXT):
        total = None
        for v in range(PTS):
            term = vec[2, POINT[v], pl.ds(o, 1), :] * pieces[v]
            total = term if total is None else total + term
        wall_ping[pl.ds(16 * o, PTS), :] = total
    pieces = [wall_ping[pl.ds(t, EXT, stride=16), :] for t in range(PTS)]
    for o in range(EXT):
        total = None
        for t in range(PTS):
            term = vec[0, POINT[t], pl.ds(o, 1), :] * pieces[t]
            total = term if total is None else total + term
        wall_pong[pl.ds(GROUP * o, EXT), :] = total
        wall_pong[pl.ds(GROUP * o + EXT, EXT), :] = total
    for copy in span_first:
        copy.wait_recv()
    contract(PTS, 1, 0, load_faces, forward(2), dense(face_ping, GROUP))
    contract(EXT, 1, 0, strided(face_ping), forward(1), dense(face_pong, GROUP))

    second_half = rows_of((GROUP, LANES)) >= EXT
    left_lanes = lanes_of((GROUP, LANES)) < LANES // 2
    third = jnp.concatenate([val[2], val[2]], axis=0)

    def halves(pick, g):
        return jnp.where(second_half, pick(2 * g + 1), pick(2 * g))

    def finish_body(g, carry):
        low = face_pong[pl.ds(g * (2 * GROUP), GROUP, stride=2), :]
        high = face_pong[pl.ds(g * (2 * GROUP) + 1, GROUP, stride=2), :]
        scale = halves(lambda b: jnp.where(left_lanes, vector(1, POINT[LOW], b), vector(1, POINT[HIGH], b)), g)
        both = third + halves(lambda b: jnp.broadcast_to(val[1, pl.ds(b, 1), :], (GROUP, LANES)), g)
        for a in range(EXT):
            spot = pl.ds(pl.multiple_of(a * SLAB + g * GROUP, 8), GROUP)
            total = part[spot, :] + scale * wall_pong[pl.ds(GROUP * a, GROUP), :]
            total = total + vector(0, POINT[LOW], a) * low + vector(0, POINT[HIGH], a) * high
            part[spot, :] = total / (jnp.broadcast_to(val[0, pl.ds(a, 1), :], (GROUP, LANES)) + both)
        return carry

    lax.fori_loop(0, EXT // 2, finish_body, 0)
    contract(EXT, EXT // 2, 0, strided(part), backward(2), dense(mixed))
    contract(EXT, EXT // 2, 0, strided(mixed), backward(1), dense(part))

    def place_points(g, o, total):
        solved[o, 2 * g, pl.ds(0, EXT), :] = total[0:EXT]
        solved[o, 2 * g + 1, pl.ds(0, EXT), :] = total[EXT:GROUP]

    last = EXT // 2 - 1
    contract(EXT, last + 1, last, strided(part), backward(0), place_points)
    blank4 = jnp.zeros((16 - EXT, LANES), f32)
    for t in range(PTS):
        solved[t, LOW, pl.ds(EXT, 16 - EXT), :] = blank4
        solved[t, HIGH, pl.ds(EXT, 16 - EXT), :] = blank4
    pack(solved, HIGH, LANES - EZ, 2)
    pack(solved, LOW, 0, 3)
    send_walls(1)

    contract(EXT, last, 0, strided(part), backward(0), place_points, (LOW, HIGH))

    span_second = [
        remote(solved.at[HIGH, inner, inner, :], face_in.at[0, :, inner, :], span_send.at[2], span_recv.at[2], "span", above),
        remote(solved.at[LOW, inner, inner, :], face_in.at[1, :, inner, :], span_send.at[3], span_recv.at[3], "span", below),
    ]
    for copy in span_second:
        copy.start()
    contract(EXT, last, 0, strided(part), backward(0), place_points, range(PTS))

    pl.when(s > 0)(coarse_solve)

    flat_solved = solved.reshape(EXT * EXT * 16, LANES)

    def stream_body(g, carry):
        def at(v):
            return pl.ds(g * (GROUP * 16) + v, GROUP, stride=16)
        low = jnp.where(inside, permute(flat_solved[at(HIGH), :], upstream), 0.0)
        high = jnp.where(inside, permute(flat_solved[at(LOW), :], downstream), 0.0)
        flat_solved[at(0), :] = flat_solved[at(0), :] + low
        flat_solved[at(PTS - 1), :] = flat_solved[at(PTS - 1), :] + high
        return carry

    lax.fori_loop(0, PTS // 2, stream_body, 0)

    receive_walls(1)
    for t in range(PTS):
        for half in range(2):
            span_rows = pl.ds(8 * half, 8)
            low = jnp.where(first_line, unpack(2, t, half, 0), turn(solved[t, HIGH, span_rows, :], EZ))
            high = jnp.where(end_line, unpack(3, t, half, LANES - EZ), turn(solved[t, LOW, span_rows, :], -EZ))
            count = 8 if half == 0 else PTS - 8
            kept = pl.ds(8 * half, count)
            solved[t, 0, kept, :] = solved[t, 0, kept, :] + low[0:count]
            solved[t, PTS - 1, kept, :] = solved[t, PTS - 1, kept, :] + high[0:count]

    def out_copy(t):
        return pltpu.make_async_copy(solved.at[t, inner, inner, :], out.at[t], out_sem.at[t])

    for t in range(1, PTS - 1):
        out_copy(t).start()
    for side, layer in ((0, 0), (1, PTS - 1)):
        span_second[side].wait_recv()

        def span_body(u, carry):
            solved[layer, u, inner, :] = solved[layer, u, inner, :] + face_in[side, u, inner, :]
            return carry

        lax.fori_loop(0, PTS, span_body, 0)
        out_copy(layer).start()

    factor, shift = divider(rows, verts)
    known = jnp.maximum(ids, 0)
    owner = (known * factor) >> shift
    local = known - owner * rows
    wanted = owner * 8 + (local >> 7)
    column_picks = (rows_of((LANES, width)) == (local & (LANES - 1))).astype(f32)
    picks = column_picks.astype(jnp.bfloat16)
    for k in range(1, walls):
        y_arrival(k).wait_recv()
    table = exact(yall[...].reshape(8 * walls, LANES), picks, ((1,), (0,)))
    found = jnp.sum(jnp.where(rows_of((8 * walls, width)) == wanted, table, 0.0), axis=0, keepdims=True)
    tops = found[:, 2 * LANES :]
    top = (tops, turn(tops, EZ))
    for a in range(2):
        base = found[:, a * LANES : (a + 1) * LANES]
        csum[0, pl.ds(2 * a, 1), :] = base
        csum[0, pl.ds(2 * a + 1, 1), :] = jnp.where(last_line, top[a], turn(base, -EZ))
    near = csum[0]
    far = permute(near, downstream8)
    csum[1] = far
    corner_copy = pltpu.make_async_copy(csum, corners_out, local_sem.at[5])
    corner_copy.start()

    for copy in span_first + span_second:
        copy.wait_send()
    finish_walls(0)
    finish_walls(1)
    for k in range(1, walls):
        x_copy(k).wait_send()
        y_copy(k).wait_send()
    for t in range(PTS):
        out_copy(t).wait()
    corner_copy.wait()


def lift(base, corners, out, held, near, low_lift, step_lift, in_sem, out_sem, near_sem):
    near_copy = pltpu.make_async_copy(corners, near, near_sem)
    near_copy.start()
    loads = [pltpu.make_async_copy(base.at[t], held.at[t], in_sem.at[t]) for t in range(PTS)]
    stores = [pltpu.make_async_copy(held.at[t], out.at[t], out_sem.at[t]) for t in range(PTS)]
    for copy in loads:
        copy.start()
    near_copy.wait()
    share = (2.0 * rows_of((PTS, LANES)).astype(f32) + 1.0) / (2 * PTS)
    across = []
    for ab in range(4):
        begin = jnp.broadcast_to(near[0, pl.ds(ab, 1), :], (PTS, LANES))
        end = jnp.broadcast_to(near[1, pl.ds(ab, 1), :], (PTS, LANES))
        across.append(begin + (end - begin) * share)
    for u in range(PTS):
        low = across[0] + (across[1] - across[0]) * upper(u)
        high = across[2] + (across[3] - across[2]) * upper(u)
        low_lift[u] = low
        step_lift[u] = high - low
    for t in range(PTS):
        loads[t].wait()
        for u in range(PTS):
            held[t, u] = held[t, u] + (low_lift[u] + step_lift[u] * upper(t))
        stores[t].start()
    for copy in stores:
        copy.wait()


def solution(mesh):
    spans, walls = mesh.shape["span"], mesh.shape["wall"]

    def per_device(residual, eig_values, eig_vectors, corner_map, stream_links, coarse_inverse):
        rows, verts = coarse_inverse.shape[1:]
        held = -(-verts // LANES)
        held = -(-held // 8) * 8
        padded = -(-rows // LANES) * LANES
        vmem = lambda *shape: pltpu.VMEM(shape, f32)
        dma = lambda count: pltpu.SemaphoreType.DMA((count,))
        base, corners = pl.pallas_call(
            functools.partial(kernel, spans, walls, verts),
            out_shape=[jax.ShapeDtypeStruct(residual.shape, f32), jax.ShapeDtypeStruct((2, 8, LANES), f32)],
            in_specs=[pl.BlockSpec(memory_space=pltpu.HBM)] * 6,
            out_specs=[pl.BlockSpec(memory_space=pl.ANY)] * 2,
            scratch_shapes=[
                vmem(PTS, EXT, 16, LANES),
                vmem(2, EXT, 16, LANES),
                vmem(PTS, 16, LANES),
                vmem(EXT * EXT * PTS, LANES),
                vmem(EXT * EXT * PTS, LANES),
                vmem(EXT * GROUP, LANES),
                vmem(EXT * GROUP, LANES),
                vmem(EXT * 16, LANES),
                vmem(EXT * GROUP, LANES),
                vmem(EXT * SLAB, LANES),
                vmem(EXT * SLAB, LANES),
                vmem(EXT, EXT, 16, LANES),
                vmem(*eig_vectors.shape),
                vmem(*eig_values.shape),
                pltpu.VMEM(corner_map.shape, jnp.int32),
                pltpu.SMEM(stream_links.shape, jnp.int32),
                vmem(rows, verts),
                vmem(2, padded, LANES),
                vmem(2, 8, LANES),
                vmem(held, LANES),
                vmem(walls, held, LANES),
                vmem(8, LANES),
                vmem(walls, 8, LANES),
                vmem(4, 24, LANES),
                vmem(4, 24, LANES),
                vmem(2, PTS, 16, LANES),
                dma(6), dma(PTS), dma(4), dma(4), dma(4), dma(4),
                dma(walls), dma(walls), dma(walls), dma(walls),
                pltpu.SemaphoreType.REGULAR((2,)),
            ],
            compiler_params=pltpu.CompilerParams(
                collective_id=0, has_side_effects=True, vmem_limit_bytes=60 * 2**20
            ),
        )(residual, eig_values, eig_vectors, corner_map, stream_links, jnp.transpose(coarse_inverse, (1, 0, 2)))
        return pl.pallas_call(
            lift,
            out_shape=jax.ShapeDtypeStruct(residual.shape, f32),
            in_specs=[pl.BlockSpec(memory_space=pltpu.HBM)] * 2,
            out_specs=pl.BlockSpec(memory_space=pl.ANY),
            scratch_shapes=[
                vmem(PTS, PTS, PTS, LANES),
                vmem(2, 8, LANES),
                vmem(PTS, PTS, LANES),
                vmem(PTS, PTS, LANES),
                dma(PTS), dma(PTS), pltpu.SemaphoreType.DMA,
            ],
            compiler_params=pltpu.CompilerParams(vmem_limit_bytes=60 * 2**20),
        )(base, corners)

    return jax.shard_map(
        per_device,
        mesh=mesh,
        in_specs=(
            P(None, None, None, ("span", "wall")),
            P(None, None, ("span", "wall")),
            P(None, None, None, ("span", "wall")),
            P(None, ("span", "wall")),
            P(),
            P("span", "wall", None),
        ),
        out_specs=P(None, None, None, ("span", "wall")),
        check_vma=False,
    )
```

```python
import functools

import jax
import jax.numpy as jnp
from jax import lax
from jax.experimental import pallas as pl
from jax.experimental.pallas import tpu as pltpu
from jax.sharding import PartitionSpec as P

PTS = 10
EXT = 12
EY = 8
EZ = 16
LANES = 128
SLAB = EXT * EXT
GROUP = 2 * EXT
POINT = tuple(range(1, PTS + 1)) + (0, EXT - 1)
LOW, HIGH = PTS, PTS + 1
precise = lax.Precision.HIGHEST
f32 = jnp.float32


def upper(index):
    return (2 * index + 1) / (2 * PTS)


def rows_of(shape):
    return lax.broadcasted_iota(jnp.int32, shape, 0)


def lanes_of(shape):
    return lax.broadcasted_iota(jnp.int32, shape, 1)


def turn(values, shift):
    return pltpu.roll(values, shift % LANES, 1)


def permute(values, index):
    return jnp.take_along_axis(values, jnp.broadcast_to(index, values.shape), axis=1)


def exact(values, picks, dims, swapped=False):
    picks = picks.astype(jnp.bfloat16)
    total = None
    for _ in range(3):
        piece = values.astype(jnp.bfloat16)
        values = values - piece.astype(f32)
        pair = (picks, piece) if swapped else (piece, picks)
        term = lax.dot_general(*pair, (dims, ((), ())), preferred_element_type=f32)
        total = term if total is None else total + term
    return total


def divider(rows, top):
    for shift in range(12, 26):
        factor = -(-(1 << shift) // rows)
        if top * factor < 1 << 31 and all((v * factor) >> shift == v // rows for v in range(top)):
            return factor, shift
    raise ValueError("no divider")


def contract(count, groups, first, load, coeff, store, outputs=range(EXT)):
    def body(group, carry):
        pieces = load(group)
        for o in outputs:
            total = None
            for i in range(count):
                term = coeff(o, i) * pieces[i]
                total = term if total is None else total + term
            store(group, o, total)
        return carry

    lax.fori_loop(first, groups, body, 0)


def kernel(
    spans, walls, verts,
    res_in, val_in, vec_in, map_in, link_in, inv_in, out, faces_out, walls_out, yall, index_out,
    field, faces, wall_face, ping, pong, face_ping, face_pong, wall_ping, wall_pong, part, mixed, divisor,
    side_first, side_second, side_third, wall_one, wall_two, wall_three, solved,
    vec, val, cmap, links, inv, acc, csum, xown, xall, yown, index, pack_out, pack_in,
    local_sem, out_sem, span_send, span_recv, wall_send, wall_recv, x_send, x_recv, y_send, y_recv, meet,
):
    s = lax.axis_index("span")
    w = lax.axis_index("wall")
    rows = verts // walls
    tiles = verts // LANES
    rest = verts - tiles * LANES
    inner = pl.ds(0, PTS)

    load_field = pltpu.make_async_copy(res_in, field.at[inner, inner, inner, :], local_sem.at[0])
    load_map = pltpu.make_async_copy(map_in, cmap, local_sem.at[1])
    load_links = pltpu.make_async_copy(link_in, links, local_sem.at[2])
    load_vec = pltpu.make_async_copy(vec_in, vec, local_sem.at[3])
    load_val = pltpu.make_async_copy(val_in, val, local_sem.at[4])
    load_inv = pltpu.make_async_copy(inv_in.at[:, 0, :], inv, local_sem.at[5])
    for copy in (load_links, load_map, load_field, load_vec, load_val):
        copy.start()

    across_count = 4 if walls == 16 else 1
    along_count = walls // across_count
    row, column = lax.div(w, across_count), lax.rem(w, across_count)

    def partner(k, sign):
        down, right = k // across_count, k % across_count
        if sign < 0:
            down, right = along_count - down, across_count - right
        return lax.rem(row + down, along_count) * across_count + lax.rem(column + right, across_count)

    def hops(k):
        down, right = k // across_count, k % across_count
        return min(down, along_count - down) + min(right, across_count - right)

    partners = sorted(range(1, walls), key=lambda k: -hops(k))

    above = lax.rem(s + 1, spans)
    below = lax.rem(s + spans - 1, spans)
    even = lax.rem(s, 2) == 0
    hears_above = jnp.logical_or(even, s == spans - 1)
    hears_below = jnp.logical_and(even, s > 0)
    speaks_above = jnp.logical_not(hears_above)
    speaks_below = jnp.logical_not(hears_below)
    early = row + column < 3
    barrier = pltpu.get_barrier_semaphore()
    for k in partners:
        pl.semaphore_signal(barrier, inc=1, device_id={"wall": partner(k, 1)})

    @pl.when(speaks_above)
    def _():
        pl.semaphore_signal(barrier, inc=1, device_id={"span": above})

    @pl.when(speaks_below)
    def _():
        pl.semaphore_signal(barrier, inc=1, device_id={"span": below})

    def remote(src, dst, send, recv, axis, peer):
        return pltpu.make_async_remote_copy(
            src_ref=src, dst_ref=dst, send_sem=send, recv_sem=recv, device_id={axis: peer}
        )

    span_first = [
        remote(res_in.at[PTS - 1], faces.at[0, inner, inner, :], span_send.at[0], span_recv.at[0], "span", above),
        remote(res_in.at[0], faces.at[1, inner, inner, :], span_send.at[1], span_recv.at[1], "span", below),
    ]
    def wall_copies(turn_index):
        base = 2 * turn_index
        landing = walls_out if turn_index else pack_in
        up = remote(pack_out.at[base], landing.at[0], wall_send.at[base], wall_recv.at[base],
                    "wall", lax.rem(w + 1, walls))
        down = remote(pack_out.at[base + 1], landing.at[1], wall_send.at[base + 1], wall_recv.at[base + 1],
                      "wall", lax.rem(w + walls - 1, walls))
        return up, down

    has_up = w < walls - 1
    has_down = w > 0

    def send_walls(turn_index):
        up, down = wall_copies(turn_index)
        pl.when(has_up)(up.start)
        pl.when(has_down)(down.start)

    def receive_walls(turn_index):
        up, down = wall_copies(turn_index)
        pl.when(has_down)(up.wait_recv)
        pl.when(has_up)(down.wait_recv)

    def finish_walls(turn_index):
        up, down = wall_copies(turn_index)
        pl.when(has_up)(up.wait_send)
        pl.when(has_down)(down.wait_send)

    lane = lanes_of((8, LANES))
    slot_of = lane // EZ

    def pack(source, lane_from, dest):
        parts = [None] * 3
        for t in range(PTS):
            for half in range(2):
                slot = 2 * t + half
                piece = source(t, half)
                place = slot % 8
                moved = turn(piece, EZ * place - lane_from)
                held = parts[slot // 8]
                parts[slot // 8] = moved if held is None else jnp.where(slot_of == place, moved, held)
        for index, part in enumerate(parts):
            pack_out[dest, pl.ds(8 * index, 8), :] = part

    def no_neighbour(side):
        return pltpu.make_async_copy(pack_in.at[side], walls_out.at[side], out_sem.at[PTS + side])

    @pl.when(jnp.logical_not(has_down))
    def _():
        pack_in[0] = jnp.zeros(pack_in.shape[1:], f32)
        no_neighbour(0).start()

    @pl.when(jnp.logical_not(has_up))
    def _():
        pack_in[1] = jnp.zeros(pack_in.shape[1:], f32)
        no_neighbour(1).start()

    blank = jnp.zeros((16 - PTS, LANES), f32)
    for t in range(PTS):
        field[t, 0, pl.ds(PTS, 16 - PTS), :] = blank
        field[t, PTS - 1, pl.ds(PTS, 16 - PTS), :] = blank
    for side in range(2):
        for u in (LOW, HIGH):
            faces[side, u] = jnp.zeros((16, LANES), f32)
    csum[...] = jnp.zeros(csum.shape, f32)
    acc[...] = jnp.zeros(acc.shape, f32)

    load_links.wait()
    lane_row = lanes_of((8, LANES))
    place = lane_row % EZ
    up_slot = jnp.zeros((8, LANES), jnp.int32)
    down_slot = jnp.zeros((8, LANES), jnp.int32)
    for q in range(EZ):
        up_slot = jnp.where(place == q, links[0, q], up_slot)
        down_slot = jnp.where(place == q, links[1, q], down_slot)
    line = lane_row - place
    upstream8 = line + up_slot
    downstream8 = line + down_slot
    upstream = jnp.concatenate([upstream8] * 3, axis=0)
    downstream = jnp.concatenate([downstream8] * 3, axis=0)

    load_field.wait()
    pack(lambda t, half: field[t, PTS - 1, pl.ds(8 * half, 8), :], LANES - EZ, 0)
    pack(lambda t, half: field[t, 0, pl.ds(8 * half, 8), :], 0, 1)
    used = pl.ds(0, tiles + (1 if rest else 0))
    width = 3 * LANES
    index_copy = pltpu.make_async_copy(index, index_out, local_sem.at[6])

    def vertex_sums():
        def corner_body(u, sums):
            total = None
            weighted = None
            for t in range(PTS):
                piece = field[t, u, inner, :]
                term = piece * upper(t)
                total = piece if total is None else total + piece
                weighted = term if weighted is None else weighted + term
            low = total - weighted
            share = (2.0 * u.astype(f32) + 1.0) / (2 * PTS)
            low_up = low * share
            high_up = weighted * share
            return (sums[0] + (low - low_up), sums[1] + low_up,
                    sums[2] + (weighted - high_up), sums[3] + high_up)

        nothing = jnp.zeros((PTS, LANES), f32)
        sums = lax.fori_loop(0, PTS, corner_body, (nothing,) * 4)
        share_v = (2.0 * rows_of((PTS, LANES)).astype(f32) + 1.0) / (2 * PTS)
        for ab in range(4):
            upper_part = sums[ab] * share_v
            csum[0, pl.ds(ab, 1), :] = jnp.sum(sums[ab] - upper_part, axis=0, keepdims=True)
            csum[1, pl.ds(ab, 1), :] = jnp.sum(upper_part, axis=0, keepdims=True)
        lines = csum[0] + permute(csum[1], upstream8)
        moved_up = jnp.where(lane >= EZ, turn(lines, EZ), 0.0)
        moved_down = turn(lines, -EZ)
        lane1 = lanes_of((1, LANES))
        last_line = lane1 >= LANES - EZ
        second_line = lane1 >= LANES - 2 * EZ
        values = jnp.concatenate([
            lines[0:1] + moved_up[1:2],
            lines[2:3] + moved_up[3:4],
            jnp.where(last_line, lines[1:2], jnp.where(second_line, moved_down[3:4], 0.0)),
        ], axis=1)

        load_map.wait()
        moved_map = turn(cmap[...], -EZ)
        ids = jnp.concatenate([
            cmap[0:1, :],
            cmap[4:5, :],
            jnp.where(last_line, cmap[2:3, :], jnp.where(second_line, moved_map[6:7], -1)),
        ], axis=1)
        index[pl.ds(0, 8), :] = jnp.broadcast_to(ids, (8, width))
        index[pl.ds(8, 8), :] = jnp.concatenate([downstream8] * 3, axis=1)
        index_copy.start()
        held = xown.shape[0]
        spread = jnp.where(rows_of((held, width)) == (ids >> 7), values, 0.0)
        onehot = (rows_of((LANES, width)) == (ids & (LANES - 1))).astype(f32)
        xown[...] = exact(spread, onehot, ((1,), (1,)))

    pl.when(early)(vertex_sums)

    greeted = walls - 1 + hears_above.astype(jnp.int32) + hears_below.astype(jnp.int32)
    pl.semaphore_wait(barrier, greeted)
    send_walls(0)

    @pl.when(hears_above)
    def _():
        pl.semaphore_signal(meet.at[1], inc=1, device_id={"span": above})

    @pl.when(hears_below)
    def _():
        pl.semaphore_signal(meet.at[0], inc=1, device_id={"span": below})

    pl.when(jnp.logical_not(early))(vertex_sums)

    def x_copy(k):
        return remote(xown.at[used], xall.at[k, used], x_send.at[k], x_recv.at[k], "wall", partner(k, 1))

    for k in partners:
        x_copy(k).start()
    pl.when(hears_above)(span_first[0].start)
    pl.when(hears_below)(span_first[1].start)
    load_inv.start()

    first_line = lane < EZ
    end_line = lane >= LANES - EZ

    def wall_body(t, carry):
        for half in range(2):
            span_rows = pl.ds(8 * half, 8)
            low = turn(field[t, PTS - 1, span_rows, :], EZ)
            field[t, LOW, span_rows, :] = jnp.where(first_line, 0.0, low)
            high = turn(field[t, 0, span_rows, :], -EZ)
            field[t, HIGH, span_rows, :] = jnp.where(end_line, 0.0, high)
        return carry

    lax.fori_loop(0, PTS, wall_body, 0)

    @pl.when(speaks_above)
    def _():
        pl.semaphore_wait(meet.at[0], 1)
        span_first[0].start()

    @pl.when(jnp.logical_not(even))
    def _():
        pl.semaphore_wait(meet.at[1], 1)
        span_first[1].start()

    def vector(direction, point, mode):
        return jnp.broadcast_to(vec[direction, point, pl.ds(mode, 1), :], (GROUP, LANES))

    def strided(ref, count=EXT):
        return lambda g: [ref[pl.ds(g * (GROUP * count) + i, GROUP, stride=count), :] for i in range(count)]

    def dense(ref, length=SLAB):
        def put(g, o, total):
            ref[pl.ds(pl.multiple_of(o * length + g * GROUP, 8), GROUP), :] = total
        return put

    load_vec.wait()
    load_val.wait()
    flat_field = field.reshape(PTS * EXT * 16, LANES)
    flat_faces = faces.reshape(2 * EXT * 16, LANES)
    inside = (rows_of((GROUP, LANES)) % EXT) < PTS

    def load_first(g):
        pieces = [flat_field[pl.ds(g * (GROUP * 16) + v, GROUP, stride=16), :] for v in range(PTS)]
        pieces.append(jnp.where(inside, permute(pieces[PTS - 1], upstream), 0.0))
        pieces.append(jnp.where(inside, permute(pieces[0], downstream), 0.0))
        return pieces

    def load_faces(g):
        return [flat_faces[pl.ds(v, GROUP, stride=16), :] for v in range(PTS)]

    forward = lambda d: lambda o, i: vector(d, POINT[i], o)
    backward = lambda d: lambda o, i: vector(d, POINT[o], i)
    short = EXT * PTS
    contract(EXT, PTS // 2, 0, load_first, forward(2), dense(ping, short))
    contract(EXT, PTS // 2, 0, strided(ping), forward(1), dense(pong, short))
    contract(PTS, EXT // 2, 0, strided(pong, PTS), forward(0), dense(part))

    second_half = rows_of((GROUP, LANES)) >= EXT
    left_lanes = lanes_of((GROUP, LANES)) < LANES // 2
    third = jnp.concatenate([val[2], val[2]], axis=0)

    def halves(pick, g):
        return jnp.where(second_half, pick(2 * g + 1), pick(2 * g))

    def divisor_body(g, carry):
        both = third + halves(lambda b: jnp.broadcast_to(val[1, pl.ds(b, 1), :], (GROUP, LANES)), g)
        for a in range(EXT):
            spot = pl.ds(pl.multiple_of(a * SLAB + g * GROUP, 8), GROUP)
            divisor[spot, :] = 1.0 / (jnp.broadcast_to(val[0, pl.ds(a, 1), :], (GROUP, LANES)) + both)
        return carry

    lax.fori_loop(0, EXT // 2, divisor_body, 0)

    @pl.when(s == 0)
    def _():
        pl.semaphore_wait(meet.at[1], 1)
        span_first[1].start()

    y_keep = pltpu.make_async_copy(yown, yall.at[w], local_sem.at[7])

    def y_copy(k):
        return remote(yown, yall.at[w], y_send.at[k], y_recv.at[k], "wall", partner(k, 1))

    def y_arrival(k):
        sender = partner(k, -1)
        return remote(yown, yall.at[sender], y_send.at[k], y_recv.at[k], "wall", sender)

    def coarse_solve():
        load_inv.wait()
        for k in range(1, walls):
            x_copy(k).wait_recv()
        total_x = xown[...]
        for k in range(1, walls):
            total_x = total_x + xall[k]
        xall[0] = total_x

        def times(start, count):
            total = None
            for c in range(tiles):
                term = inv[pl.ds(start, count), pl.ds(c * LANES, LANES)] * xall[0, pl.ds(c, 1), :]
                total = term if total is None else total + term
            acc[0, pl.ds(start, count), :] = total
            if rest:
                tail = inv[pl.ds(start, count), pl.ds(tiles * LANES, rest)] * xall[0, pl.ds(tiles, 1), pl.ds(0, rest)]
                acc[1, pl.ds(start, count), pl.ds(0, rest)] = tail

        chunk = 32
        whole = rows // chunk

        def times_body(r, carry):
            times(pl.multiple_of(r * chunk, chunk), chunk)
            return carry

        lax.fori_loop(0, whole, times_body, 0)
        if rows - whole * chunk:
            times(whole * chunk, rows - whole * chunk)
        ones = jnp.ones((8, LANES), f32)
        own = exact(acc[0] + acc[1], ones, ((1,), (1,)), True)
        row8 = rows_of((8, LANES))
        tile = own[:, 0:LANES]
        for part in range(1, acc.shape[1] // LANES):
            tile = jnp.where(row8 == part, own[:, part * LANES : (part + 1) * LANES], tile)
        yown[...] = tile
        y_keep.start()

        for k in partners:
            y_copy(k).start()

    pl.when(s == 0)(coarse_solve)

    receive_walls(0)
    for t in range(PTS):
        for half in range(2):
            kept = jnp.where(end_line, unpack(pack_in, 1, t, half, LANES - EZ), 0.0)
            wall_face[t, pl.ds(8 * half, 8), :] = jnp.where(first_line, unpack(pack_in, 0, t, half, 0), kept)
    flat_wall = wall_face.reshape(PTS * 16, LANES)
    pieces = [flat_wall[pl.ds(v, PTS, stride=16), :] for v in range(PTS)]
    for o in range(EXT):
        total = None
        for v in range(PTS):
            term = vec[2, POINT[v], pl.ds(o, 1), :] * pieces[v]
            total = term if total is None else total + term
        wall_ping[pl.ds(16 * o, PTS), :] = total
    pieces = [wall_ping[pl.ds(t, EXT, stride=16), :] for t in range(PTS)]
    for o in range(EXT):
        total = None
        for t in range(PTS):
            term = vec[0, POINT[t], pl.ds(o, 1), :] * pieces[t]
            total = term if total is None else total + term
        wall_pong[pl.ds(GROUP * o, EXT), :] = total
        wall_pong[pl.ds(GROUP * o + EXT, EXT), :] = total
    for copy in span_first:
        copy.wait_recv()
    contract(PTS, 1, 0, load_faces, forward(2), dense(face_ping, GROUP))
    contract(EXT, 1, 0, strided(face_ping), forward(1), dense(face_pong, GROUP))

    def finish_body(g, carry):
        low = face_pong[pl.ds(g * (2 * GROUP), GROUP, stride=2), :]
        high = face_pong[pl.ds(g * (2 * GROUP) + 1, GROUP, stride=2), :]
        scale = halves(lambda b: jnp.where(left_lanes, vector(1, POINT[LOW], b), vector(1, POINT[HIGH], b)), g)
        for a in range(EXT):
            spot = pl.ds(pl.multiple_of(a * SLAB + g * GROUP, 8), GROUP)
            total = part[spot, :] + scale * wall_pong[pl.ds(GROUP * a, GROUP), :]
            total = total + vector(0, POINT[LOW], a) * low + vector(0, POINT[HIGH], a) * high
            part[spot, :] = total * divisor[spot, :]
        return carry

    lax.fori_loop(0, EXT // 2, finish_body, 0)
    def contract_small(pieces, coeff, outputs, store):
        for o in outputs:
            total = None
            for i in range(EXT):
                term = coeff(o, i) * pieces[i]
                total = term if total is None else total + term
            store(o, total)

    def entry(direction, point, mode):
        return vec[direction, point, pl.ds(mode, 1), :]

    def slabs(g):
        return [part[pl.ds(pl.multiple_of(a * SLAB + g * GROUP, 8), GROUP), :] for a in range(EXT)]

    def put_side(g, o, total):
        side_first[pl.ds(pl.multiple_of((o - PTS) * SLAB + g * GROUP, 8), GROUP), :] = total

    contract(EXT, EXT // 2, 0, slabs, backward(0), put_side, (LOW, HIGH))
    for side in range(2):
        def put_second(o, total):
            side_second[pl.ds(16 * o, EXT), :] = total

        def put_third(o, total):
            side_third[side, o, pl.ds(0, EXT), :] = total

        pieces = [side_first[pl.ds(side * SLAB + c, EXT, stride=EXT), :] for c in range(EXT)]
        contract_small(pieces, lambda o, i: entry(2, POINT[o], i), range(EXT), put_second)
        pieces = [side_second[pl.ds(b, EXT, stride=16), :] for b in range(EXT)]
        contract_small(pieces, lambda o, i: entry(1, POINT[o], i), range(PTS), put_third)
    span_second = [
        remote(side_third.at[1, :, inner, :], faces_out.at[0], span_send.at[2], span_recv.at[2], "span", above),
        remote(side_third.at[0, :, inner, :], faces_out.at[1], span_send.at[3], span_recv.at[3], "span", below),
    ]
    for copy in span_second:
        copy.start()

    def wall_first(a, carry):
        pieces = [part[pl.ds(a * SLAB + b * EXT, EXT), :] for b in range(EXT)]

        def put(o, total):
            wall_one[pl.ds((o - PTS) * SLAB + a * EXT, EXT), :] = total

        contract_small(pieces, lambda o, i: entry(1, POINT[o], i), (LOW, HIGH), put)
        return carry

    lax.fori_loop(0, EXT, wall_first, 0)
    contract(EXT, 1, 0, strided(wall_one), backward(2), dense(wall_two, GROUP))
    wall_three[pl.ds(PTS * GROUP, 16), :] = jnp.zeros((16, LANES), f32)
    contract(EXT, 1, 0, strided(wall_two), backward(0), dense(wall_three, GROUP), range(PTS))

    def wall_layer(t, half, layer):
        return wall_three[pl.ds(t * GROUP + 16 * half + (layer - PTS), 8, stride=2), :]

    pack(lambda t, half: wall_layer(t, half, HIGH), LANES - EZ, 2)
    pack(lambda t, half: wall_layer(t, half, LOW), 0, 3)
    send_walls(1)

    contract(EXT, EXT // 2, 0, strided(part), backward(2), dense(mixed))
    pl.when(s > 0)(coarse_solve)
    contract(EXT, EXT // 2, 0, strided(mixed), backward(1), dense(part), range(PTS))

    def place_points(g, o, total):
        solved[o, 2 * g, pl.ds(0, EXT), :] = total[0:EXT]
        solved[o, 2 * g + 1, pl.ds(0, EXT), :] = total[EXT:GROUP]

    contract(EXT, PTS // 2, 0, strided(part), backward(0), place_points, range(PTS))

    flat_solved = solved.reshape(PTS * EXT * 16, LANES)

    def stream_body(g, carry):
        def at(v):
            return pl.ds(g * (GROUP * 16) + v, GROUP, stride=16)
        low = jnp.where(inside, permute(flat_solved[at(HIGH), :], upstream), 0.0)
        high = jnp.where(inside, permute(flat_solved[at(LOW), :], downstream), 0.0)
        flat_solved[at(0), :] = flat_solved[at(0), :] + low
        flat_solved[at(PTS - 1), :] = flat_solved[at(PTS - 1), :] + high
        return carry

    lax.fori_loop(0, PTS // 2, stream_body, 0)

    def own_walls(t, carry):
        for half in range(2):
            span_rows = pl.ds(8 * half, 8)
            low = jnp.where(first_line, 0.0, turn(wall_layer(t, half, HIGH), EZ))
            high = jnp.where(end_line, 0.0, turn(wall_layer(t, half, LOW), -EZ))
            count = 8 if half == 0 else PTS - 8
            kept = pl.ds(8 * half, count)
            solved[t, 0, kept, :] = solved[t, 0, kept, :] + low[0:count]
            solved[t, PTS - 1, kept, :] = solved[t, PTS - 1, kept, :] + high[0:count]
        return carry

    lax.fori_loop(0, PTS, own_walls, 0)

    def out_copy(t):
        return pltpu.make_async_copy(solved.at[t, inner, inner, :], out.at[t], out_sem.at[t])

    for t in range(PTS):
        out_copy(t).start()
    index_copy.wait()

    @pl.when(jnp.logical_not(has_down))
    def _():
        no_neighbour(0).wait()

    @pl.when(jnp.logical_not(has_up))
    def _():
        no_neighbour(1).wait()

    receive_walls(1)
    for copy in span_second:
        copy.wait_recv()
    for k in range(1, walls):
        y_arrival(k).wait_recv()
    y_keep.wait()
    for copy in span_first + span_second:
        copy.wait_send()
    finish_walls(0)
    finish_walls(1)
    for k in range(1, walls):
        x_copy(k).wait_send()
        y_copy(k).wait_send()
    for t in range(PTS):
        out_copy(t).wait()


def unpack(packed, side, t, half, lane_to):
    slot = 2 * t + half
    part = packed[side, pl.ds(8 * (slot // 8), 8), :]
    return turn(part, lane_to - EZ * (slot % 8))


def lift(
    rows, verts, base, faces, packed, values, index, out,
    held, faces_here, packed_here, values_here, index_here, near, low_lift, step_lift, in_sem, out_sem, small_sem,
):
    smalls = [
        pltpu.make_async_copy(there, here, small_sem.at[k])
        for k, (there, here) in enumerate((
            (index, index_here), (values, values_here), (packed, packed_here), (faces, faces_here)
        ))
    ]
    loads = [pltpu.make_async_copy(base.at[t], held.at[t], in_sem.at[t]) for t in range(PTS)]
    stores = [pltpu.make_async_copy(held.at[t], out.at[t], out_sem.at[t]) for t in range(PTS)]
    order = tuple(range(1, PTS - 1)) + (0, PTS - 1)
    for copy in smalls[:3] + [loads[t] for t in order[:-2]] + smalls[3:] + [loads[t] for t in order[-2:]]:
        copy.start()
    smalls[0].wait()
    width = 3 * LANES
    count = values_here.shape[0] * 8
    ids = index_here[pl.ds(0, 1), :]
    downstream8 = index_here[pl.ds(8, 8), pl.ds(0, LANES)]
    factor, shift = divider(rows, verts)
    known = jnp.maximum(ids, 0)
    owner = (known * factor) >> shift
    local = known - owner * rows
    wanted = owner * 8 + (local >> 7)
    picks = (rows_of((LANES, width)) == (local & (LANES - 1))).astype(f32).astype(jnp.bfloat16)
    smalls[1].wait()
    table = exact(values_here[...].reshape(count, LANES), picks, ((1,), (0,)))
    found = jnp.sum(jnp.where(rows_of((count, width)) == wanted, table, 0.0), axis=0, keepdims=True)
    last_line = lanes_of((1, LANES)) >= LANES - EZ
    tops = found[:, 2 * LANES :]
    top = (tops, turn(tops, EZ))
    near[...] = jnp.zeros(near.shape, f32)
    for a in range(2):
        row = found[:, a * LANES : (a + 1) * LANES]
        near[pl.ds(2 * a, 1), :] = row
        near[pl.ds(2 * a + 1, 1), :] = jnp.where(last_line, top[a], turn(row, -EZ))
    begins = near[...]
    ends = permute(begins, downstream8)
    share = (2.0 * rows_of((PTS, LANES)).astype(f32) + 1.0) / (2 * PTS)
    across = []
    for ab in range(4):
        begin = jnp.broadcast_to(begins[ab : ab + 1], (PTS, LANES))
        end = jnp.broadcast_to(ends[ab : ab + 1], (PTS, LANES))
        across.append(begin + (end - begin) * share)
    for u in range(PTS):
        low = across[0] + (across[1] - across[0]) * upper(u)
        high = across[2] + (across[3] - across[2]) * upper(u)
        low_lift[u] = low
        step_lift[u] = high - low
    smalls[2].wait()
    first_line = lanes_of((8, LANES)) < EZ
    end_line = lanes_of((8, LANES)) >= LANES - EZ
    for t in order:
        loads[t].wait()
        for u in range(PTS):
            held[t, u] = held[t, u] + (low_lift[u] + step_lift[u] * upper(t))
        for half in range(2):
            size = 8 if half == 0 else PTS - 8
            kept = pl.ds(8 * half, size)
            low = jnp.where(first_line, unpack(packed_here, 0, t, half, 0), 0.0)
            high = jnp.where(end_line, unpack(packed_here, 1, t, half, LANES - EZ), 0.0)
            held[t, 0, kept, :] = held[t, 0, kept, :] + low[0:size]
            held[t, PTS - 1, kept, :] = held[t, PTS - 1, kept, :] + high[0:size]
        if t in (0, PTS - 1):
            side = 0 if t == 0 else 1
            if t == 0:
                smalls[3].wait()
            for u in range(PTS):
                held[t, u] = held[t, u] + faces_here[side, u]
        stores[t].start()
    for copy in stores:
        copy.wait()


def solution(mesh):
    spans, walls = mesh.shape["span"], mesh.shape["wall"]

    def per_device(residual, eig_values, eig_vectors, corner_map, stream_links, coarse_inverse):
        rows, verts = coarse_inverse.shape[1:]
        held = -(-verts // LANES)
        held = -(-held // 8) * 8
        padded = -(-rows // LANES) * LANES
        vmem = lambda *shape: pltpu.VMEM(shape, f32)
        dma = lambda count: pltpu.SemaphoreType.DMA((count,))
        shapes = [
            jax.ShapeDtypeStruct(residual.shape, f32),
            jax.ShapeDtypeStruct((2, PTS, PTS, LANES), f32),
            jax.ShapeDtypeStruct((2, 24, LANES), f32),
            jax.ShapeDtypeStruct((walls, 8, LANES), f32),
            jax.ShapeDtypeStruct((16, 3 * LANES), jnp.int32),
        ]
        parts = pl.pallas_call(
            functools.partial(kernel, spans, walls, verts),
            out_shape=shapes,
            in_specs=[pl.BlockSpec(memory_space=pltpu.HBM)] * 6,
            out_specs=[pl.BlockSpec(memory_space=pl.ANY)] * 5,
            scratch_shapes=[
                vmem(PTS, EXT, 16, LANES),
                vmem(2, EXT, 16, LANES),
                vmem(PTS, 16, LANES),
                vmem(EXT * EXT * PTS, LANES),
                vmem(EXT * EXT * PTS, LANES),
                vmem(EXT * GROUP, LANES),
                vmem(EXT * GROUP, LANES),
                vmem(EXT * 16, LANES),
                vmem(EXT * GROUP, LANES),
                vmem(EXT * SLAB, LANES),
                vmem(EXT * SLAB, LANES),
                vmem(EXT * SLAB, LANES),
                vmem(2 * SLAB, LANES),
                vmem(EXT * 16, LANES),
                vmem(2, PTS, 16, LANES),
                vmem(2 * SLAB, LANES),
                vmem(EXT * GROUP, LANES),
                vmem(PTS * GROUP + 16, LANES),
                vmem(PTS, EXT, 16, LANES),
                vmem(*eig_vectors.shape),
                vmem(*eig_values.shape),
                pltpu.VMEM(corner_map.shape, jnp.int32),
                pltpu.SMEM(stream_links.shape, jnp.int32),
                vmem(rows, verts),
                vmem(2, padded, LANES),
                vmem(2, 8, LANES),
                vmem(held, LANES),
                vmem(walls, held, LANES),
                vmem(8, LANES),
                pltpu.VMEM((16, 3 * LANES), jnp.int32),
                vmem(4, 24, LANES),
                vmem(2, 24, LANES),
                dma(8), dma(PTS + 2), dma(4), dma(4), dma(4), dma(4),
                dma(walls), dma(walls), dma(walls), dma(walls),
                pltpu.SemaphoreType.REGULAR((2,)),
            ],
            compiler_params=pltpu.CompilerParams(
                collective_id=0, has_side_effects=True, vmem_limit_bytes=60 * 2**20
            ),
        )(residual, eig_values, eig_vectors, corner_map, stream_links, jnp.transpose(coarse_inverse, (1, 0, 2)))
        return pl.pallas_call(
            functools.partial(lift, rows, verts),
            out_shape=jax.ShapeDtypeStruct(residual.shape, f32),
            in_specs=[pl.BlockSpec(memory_space=pltpu.HBM)] * 5,
            out_specs=pl.BlockSpec(memory_space=pl.ANY),
            scratch_shapes=[
                vmem(*residual.shape),
                vmem(2, PTS, PTS, LANES),
                vmem(2, 24, LANES),
                vmem(walls, 8, LANES),
                pltpu.VMEM((16, 3 * LANES), jnp.int32),
                vmem(8, LANES),
                vmem(PTS, PTS, LANES),
                vmem(PTS, PTS, LANES),
                dma(PTS), dma(PTS), dma(4),
            ],
            compiler_params=pltpu.CompilerParams(vmem_limit_bytes=60 * 2**20),
        )(*parts)

    return jax.shard_map(
        per_device,
        mesh=mesh,
        in_specs=(
            P(None, None, None, ("span", "wall")),
            P(None, None, ("span", "wall")),
            P(None, None, None, ("span", "wall")),
            P(None, ("span", "wall")),
            P(),
            P("span", "wall", None),
        ),
        out_specs=P(None, None, None, ("span", "wall")),
        check_vma=False,
    )
```

```python
import functools

import jax
import jax.numpy as jnp
from jax import lax
from jax.experimental import pallas as pl
from jax.experimental.pallas import tpu as pltpu
from jax.sharding import PartitionSpec as P

PTS = 10
EXT = 12
EY = 8
EZ = 16
LANES = 128
SLAB = EXT * EXT
GROUP = 2 * EXT
POINT = tuple(range(1, PTS + 1)) + (0, EXT - 1)
LOW, HIGH = PTS, PTS + 1
precise = lax.Precision.HIGHEST
f32 = jnp.float32


def upper(index):
    return (2 * index + 1) / (2 * PTS)


def rows_of(shape):
    return lax.broadcasted_iota(jnp.int32, shape, 0)


def lanes_of(shape):
    return lax.broadcasted_iota(jnp.int32, shape, 1)


def turn(values, shift):
    return pltpu.roll(values, shift % LANES, 1)


def permute(values, index):
    return jnp.take_along_axis(values, jnp.broadcast_to(index, values.shape), axis=1)


def exact(values, picks, dims, swapped=False):
    picks = picks.astype(jnp.bfloat16)
    total = None
    for _ in range(3):
        piece = values.astype(jnp.bfloat16)
        values = values - piece.astype(f32)
        pair = (picks, piece) if swapped else (piece, picks)
        term = lax.dot_general(*pair, (dims, ((), ())), preferred_element_type=f32)
        total = term if total is None else total + term
    return total


def divider(rows, top):
    for shift in range(12, 26):
        factor = -(-(1 << shift) // rows)
        if top * factor < 1 << 31 and all((v * factor) >> shift == v // rows for v in range(top)):
            return factor, shift
    raise ValueError("no divider")


def contract(count, groups, first, load, coeff, store, outputs=range(EXT)):
    def body(group, carry):
        pieces = load(group)
        for o in outputs:
            total = None
            for i in range(count):
                term = coeff(o, i) * pieces[i]
                total = term if total is None else total + term
            store(group, o, total)
        return carry

    lax.fori_loop(first, groups, body, 0)


def kernel(
    spans, walls, verts,
    res_in, val_in, vec_in, map_in, link_in, inv_in, out, faces_out, walls_out, yall, index_out,
    field, faces, wall_face, ping, pong, face_ping, face_pong, wall_ping, wall_pong, part, mixed, divisor,
    side_first, side_second, side_third, wall_one, wall_two, wall_three, solved,
    vec, val, cmap, links, inv, acc, csum, xown, xall, yown, index, pack_out, pack_in,
    local_sem, out_sem, span_send, span_recv, wall_send, wall_recv, x_send, x_recv, y_send, y_recv, meet,
):
    s = lax.axis_index("span")
    w = lax.axis_index("wall")
    rows = verts // walls
    tiles = verts // LANES
    rest = verts - tiles * LANES
    inner = pl.ds(0, PTS)

    load_field = pltpu.make_async_copy(res_in, field.at[inner, inner, inner, :], local_sem.at[0])
    load_map = pltpu.make_async_copy(map_in, cmap, local_sem.at[1])
    load_links = pltpu.make_async_copy(link_in, links, local_sem.at[2])
    load_vec = pltpu.make_async_copy(vec_in, vec, local_sem.at[3])
    load_val = pltpu.make_async_copy(val_in, val, local_sem.at[4])
    load_inv = pltpu.make_async_copy(inv_in.at[:, 0, :], inv, local_sem.at[5])
    for copy in (load_links, load_map, load_field, load_vec, load_val):
        copy.start()

    across_count = 4 if walls == 16 else 1
    along_count = walls // across_count
    row, column = lax.div(w, across_count), lax.rem(w, across_count)

    def partner(k, sign):
        down, right = k // across_count, k % across_count
        if sign < 0:
            down, right = along_count - down, across_count - right
        return lax.rem(row + down, along_count) * across_count + lax.rem(column + right, across_count)

    def hops(k):
        down, right = k // across_count, k % across_count
        return min(down, along_count - down) + min(right, across_count - right)

    partners = sorted(range(1, walls), key=lambda k: -hops(k))

    above = lax.rem(s + 1, spans)
    below = lax.rem(s + spans - 1, spans)
    even = lax.rem(s, 2) == 0
    hears_above = jnp.logical_or(even, s == spans - 1)
    hears_below = jnp.logical_and(even, s > 0)
    speaks_above = jnp.logical_not(hears_above)
    speaks_below = jnp.logical_not(hears_below)
    early = row + column < 3
    barrier = pltpu.get_barrier_semaphore()
    for k in partners:
        pl.semaphore_signal(barrier, inc=1, device_id={"wall": partner(k, 1)})

    @pl.when(speaks_above)
    def _():
        pl.semaphore_signal(barrier, inc=1, device_id={"span": above})

    @pl.when(speaks_below)
    def _():
        pl.semaphore_signal(barrier, inc=1, device_id={"span": below})

    def remote(src, dst, send, recv, axis, peer):
        return pltpu.make_async_remote_copy(
            src_ref=src, dst_ref=dst, send_sem=send, recv_sem=recv, device_id={axis: peer}
        )

    span_first = [
        remote(res_in.at[PTS - 1], faces.at[0, inner, inner, :], span_send.at[0], span_recv.at[0], "span", above),
        remote(res_in.at[0], faces.at[1, inner, inner, :], span_send.at[1], span_recv.at[1], "span", below),
    ]
    def wall_copies(turn_index):
        base = 2 * turn_index
        landing = walls_out if turn_index else pack_in
        up = remote(pack_out.at[base], landing.at[0], wall_send.at[base], wall_recv.at[base],
                    "wall", lax.rem(w + 1, walls))
        down = remote(pack_out.at[base + 1], landing.at[1], wall_send.at[base + 1], wall_recv.at[base + 1],
                      "wall", lax.rem(w + walls - 1, walls))
        return up, down

    has_up = w < walls - 1
    has_down = w > 0

    def send_walls(turn_index):
        up, down = wall_copies(turn_index)
        pl.when(has_up)(up.start)
        pl.when(has_down)(down.start)

    def receive_walls(turn_index):
        up, down = wall_copies(turn_index)
        pl.when(has_down)(up.wait_recv)
        pl.when(has_up)(down.wait_recv)

    def finish_walls(turn_index):
        up, down = wall_copies(turn_index)
        pl.when(has_up)(up.wait_send)
        pl.when(has_down)(down.wait_send)

    lane = lanes_of((8, LANES))
    slot_of = lane // EZ

    def pack(source, lane_from, dest):
        parts = [None] * 3
        for t in range(PTS):
            for half in range(2):
                slot = 2 * t + half
                piece = source(t, half)
                place = slot % 8
                moved = turn(piece, EZ * place - lane_from)
                held = parts[slot // 8]
                parts[slot // 8] = moved if held is None else jnp.where(slot_of == place, moved, held)
        for index, part in enumerate(parts):
            pack_out[dest, pl.ds(8 * index, 8), :] = part

    def no_neighbour(side):
        return pltpu.make_async_copy(pack_in.at[side], walls_out.at[side], out_sem.at[PTS + side])

    @pl.when(jnp.logical_not(has_down))
    def _():
        pack_in[0] = jnp.zeros(pack_in.shape[1:], f32)
        no_neighbour(0).start()

    @pl.when(jnp.logical_not(has_up))
    def _():
        pack_in[1] = jnp.zeros(pack_in.shape[1:], f32)
        no_neighbour(1).start()

    blank = jnp.zeros((16 - PTS, LANES), f32)
    for t in range(PTS):
        field[t, 0, pl.ds(PTS, 16 - PTS), :] = blank
        field[t, PTS - 1, pl.ds(PTS, 16 - PTS), :] = blank
    for side in range(2):
        for u in (LOW, HIGH):
            faces[side, u] = jnp.zeros((16, LANES), f32)
    csum[...] = jnp.zeros(csum.shape, f32)
    acc[...] = jnp.zeros(acc.shape, f32)

    load_links.wait()
    lane_row = lanes_of((8, LANES))
    place = lane_row % EZ
    up_slot = jnp.zeros((8, LANES), jnp.int32)
    down_slot = jnp.zeros((8, LANES), jnp.int32)
    for q in range(EZ):
        up_slot = jnp.where(place == q, links[0, q], up_slot)
        down_slot = jnp.where(place == q, links[1, q], down_slot)
    line = lane_row - place
    upstream8 = line + up_slot
    downstream8 = line + down_slot
    upstream = jnp.concatenate([upstream8] * 3, axis=0)
    downstream = jnp.concatenate([downstream8] * 3, axis=0)

    load_field.wait()
    pack(lambda t, half: field[t, PTS - 1, pl.ds(8 * half, 8), :], LANES - EZ, 0)
    pack(lambda t, half: field[t, 0, pl.ds(8 * half, 8), :], 0, 1)
    used = pl.ds(0, tiles + (1 if rest else 0))
    width = 3 * LANES
    index_copy = pltpu.make_async_copy(index, index_out, local_sem.at[6])

    def vertex_sums():
        def corner_body(u, sums):
            total = None
            weighted = None
            for t in range(PTS):
                piece = field[t, u, inner, :]
                term = piece * upper(t)
                total = piece if total is None else total + piece
                weighted = term if weighted is None else weighted + term
            low = total - weighted
            share = (2.0 * u.astype(f32) + 1.0) / (2 * PTS)
            low_up = low * share
            high_up = weighted * share
            return (sums[0] + (low - low_up), sums[1] + low_up,
                    sums[2] + (weighted - high_up), sums[3] + high_up)

        nothing = jnp.zeros((PTS, LANES), f32)
        sums = lax.fori_loop(0, PTS, corner_body, (nothing,) * 4)
        share_v = (2.0 * rows_of((PTS, LANES)).astype(f32) + 1.0) / (2 * PTS)
        for ab in range(4):
            upper_part = sums[ab] * share_v
            csum[0, pl.ds(ab, 1), :] = jnp.sum(sums[ab] - upper_part, axis=0, keepdims=True)
            csum[1, pl.ds(ab, 1), :] = jnp.sum(upper_part, axis=0, keepdims=True)
        lines = csum[0] + permute(csum[1], upstream8)
        moved_up = jnp.where(lane >= EZ, turn(lines, EZ), 0.0)
        moved_down = turn(lines, -EZ)
        lane1 = lanes_of((1, LANES))
        last_line = lane1 >= LANES - EZ
        second_line = lane1 >= LANES - 2 * EZ
        values = jnp.concatenate([
            lines[0:1] + moved_up[1:2],
            lines[2:3] + moved_up[3:4],
            jnp.where(last_line, lines[1:2], jnp.where(second_line, moved_down[3:4], 0.0)),
        ], axis=1)

        load_map.wait()
        moved_map = turn(cmap[...], -EZ)
        ids = jnp.concatenate([
            cmap[0:1, :],
            cmap[4:5, :],
            jnp.where(last_line, cmap[2:3, :], jnp.where(second_line, moved_map[6:7], -1)),
        ], axis=1)
        index[pl.ds(0, 8), :] = jnp.broadcast_to(ids, (8, width))
        index[pl.ds(8, 8), :] = jnp.concatenate([downstream8] * 3, axis=1)
        index_copy.start()
        held = xown.shape[0]
        spread = jnp.where(rows_of((held, width)) == (ids >> 7), values, 0.0)
        onehot = (rows_of((LANES, width)) == (ids & (LANES - 1))).astype(f32)
        xown[...] = exact(spread, onehot, ((1,), (1,)))

    pl.when(early)(vertex_sums)

    greeted = walls - 1 + hears_above.astype(jnp.int32) + hears_below.astype(jnp.int32)
    pl.semaphore_wait(barrier, greeted)
    send_walls(0)

    @pl.when(hears_above)
    def _():
        pl.semaphore_signal(meet.at[1], inc=1, device_id={"span": above})

    @pl.when(hears_below)
    def _():
        pl.semaphore_signal(meet.at[0], inc=1, device_id={"span": below})

    pl.when(jnp.logical_not(early))(vertex_sums)

    def x_copy(k):
        return remote(xown.at[used], xall.at[k, used], x_send.at[k], x_recv.at[k], "wall", partner(k, 1))

    for k in partners:
        x_copy(k).start()
    pl.when(hears_above)(span_first[0].start)
    pl.when(hears_below)(span_first[1].start)
    load_inv.start()

    first_line = lane < EZ
    end_line = lane >= LANES - EZ

    def wall_body(t, carry):
        for half in range(2):
            span_rows = pl.ds(8 * half, 8)
            low = turn(field[t, PTS - 1, span_rows, :], EZ)
            field[t, LOW, span_rows, :] = jnp.where(first_line, 0.0, low)
            high = turn(field[t, 0, span_rows, :], -EZ)
            field[t, HIGH, span_rows, :] = jnp.where(end_line, 0.0, high)
        return carry

    lax.fori_loop(0, PTS, wall_body, 0)

    @pl.when(speaks_above)
    def _():
        pl.semaphore_wait(meet.at[0], 1)
        span_first[0].start()

    @pl.when(jnp.logical_not(even))
    def _():
        pl.semaphore_wait(meet.at[1], 1)
        span_first[1].start()

    def vector(direction, point, mode):
        return jnp.broadcast_to(vec[direction, point, pl.ds(mode, 1), :], (GROUP, LANES))

    def strided(ref, count=EXT):
        return lambda g: [ref[pl.ds(g * (GROUP * count) + i, GROUP, stride=count), :] for i in range(count)]

    def dense(ref, length=SLAB):
        def put(g, o, total):
            ref[pl.ds(pl.multiple_of(o * length + g * GROUP, 8), GROUP), :] = total
        return put

    load_vec.wait()
    load_val.wait()
    flat_field = field.reshape(PTS * EXT * 16, LANES)
    flat_faces = faces.reshape(2 * EXT * 16, LANES)
    inside = (rows_of((GROUP, LANES)) % EXT) < PTS

    def load_first(g):
        pieces = [flat_field[pl.ds(g * (GROUP * 16) + v, GROUP, stride=16), :] for v in range(PTS)]
        pieces.append(jnp.where(inside, permute(pieces[PTS - 1], upstream), 0.0))
        pieces.append(jnp.where(inside, permute(pieces[0], downstream), 0.0))
        return pieces

    def load_faces(g):
        return [flat_faces[pl.ds(v, GROUP, stride=16), :] for v in range(PTS)]

    forward = lambda d: lambda o, i: vector(d, POINT[i], o)
    backward = lambda d: lambda o, i: vector(d, POINT[o], i)
    short = EXT * PTS
    contract(EXT, PTS // 2, 0, load_first, forward(2), dense(ping, short))
    contract(EXT, PTS // 2, 0, strided(ping), forward(1), dense(pong, short))
    contract(PTS, EXT // 2, 0, strided(pong, PTS), forward(0), dense(part))

    second_half = rows_of((GROUP, LANES)) >= EXT
    left_lanes = lanes_of((GROUP, LANES)) < LANES // 2
    third = jnp.concatenate([val[2], val[2]], axis=0)

    def halves(pick, g):
        return jnp.where(second_half, pick(2 * g + 1), pick(2 * g))

    def divisor_body(g, carry):
        both = third + halves(lambda b: jnp.broadcast_to(val[1, pl.ds(b, 1), :], (GROUP, LANES)), g)
        for a in range(EXT):
            spot = pl.ds(pl.multiple_of(a * SLAB + g * GROUP, 8), GROUP)
            divisor[spot, :] = 1.0 / (jnp.broadcast_to(val[0, pl.ds(a, 1), :], (GROUP, LANES)) + both)
        return carry

    lax.fori_loop(0, EXT // 2, divisor_body, 0)

    @pl.when(s == 0)
    def _():
        pl.semaphore_wait(meet.at[1], 1)
        span_first[1].start()

    y_keep = pltpu.make_async_copy(yown, yall.at[w], local_sem.at[7])

    def y_copy(k):
        return remote(yown, yall.at[w], y_send.at[k], y_recv.at[k], "wall", partner(k, 1))

    def y_arrival(k):
        sender = partner(k, -1)
        return remote(yown, yall.at[sender], y_send.at[k], y_recv.at[k], "wall", sender)

    def coarse_solve():
        load_inv.wait()
        for k in range(1, walls):
            x_copy(k).wait_recv()
        total_x = xown[...]
        for k in range(1, walls):
            total_x = total_x + xall[k]
        xall[0] = total_x

        def times(start, count, ways):
            sums = [None] * ways
            for c in range(tiles):
                term = inv[pl.ds(start, count), pl.ds(c * LANES, LANES)] * xall[0, pl.ds(c, 1), :]
                held = sums[c % ways]
                sums[c % ways] = term if held is None else held + term
            total = sums[0]
            for part_sum in sums[1:]:
                total = total + part_sum
            acc[0, pl.ds(start, count), :] = total
            if rest:
                tail = inv[pl.ds(start, count), pl.ds(tiles * LANES, rest)] * xall[0, pl.ds(tiles, 1), pl.ds(0, rest)]
                acc[1, pl.ds(start, count), pl.ds(0, rest)] = tail

        chunk = 64
        whole = rows // chunk

        def times_body(r, carry):
            times(pl.multiple_of(r * chunk, chunk), chunk, 2)
            return carry

        lax.fori_loop(0, whole, times_body, 0)
        if rows - whole * chunk:
            times(whole * chunk, rows - whole * chunk, 8)
        ones = jnp.ones((8, LANES), f32)
        own = exact(acc[0] + acc[1], ones, ((1,), (1,)), True)
        row8 = rows_of((8, LANES))
        tile = own[:, 0:LANES]
        for part in range(1, acc.shape[1] // LANES):
            tile = jnp.where(row8 == part, own[:, part * LANES : (part + 1) * LANES], tile)
        yown[...] = tile
        y_keep.start()

        for k in partners:
            y_copy(k).start()

    pl.when(s == 0)(coarse_solve)

    receive_walls(0)
    for t in range(PTS):
        for half in range(2):
            kept = jnp.where(end_line, unpack(pack_in, 1, t, half, LANES - EZ), 0.0)
            wall_face[t, pl.ds(8 * half, 8), :] = jnp.where(first_line, unpack(pack_in, 0, t, half, 0), kept)
    flat_wall = wall_face.reshape(PTS * 16, LANES)
    pieces = [flat_wall[pl.ds(v, PTS, stride=16), :] for v in range(PTS)]
    for o in range(EXT):
        total = None
        for v in range(PTS):
            term = vec[2, POINT[v], pl.ds(o, 1), :] * pieces[v]
            total = term if total is None else total + term
        wall_ping[pl.ds(16 * o, PTS), :] = total
    pieces = [wall_ping[pl.ds(t, EXT, stride=16), :] for t in range(PTS)]
    for o in range(EXT):
        total = None
        for t in range(PTS):
            term = vec[0, POINT[t], pl.ds(o, 1), :] * pieces[t]
            total = term if total is None else total + term
        wall_pong[pl.ds(GROUP * o, EXT), :] = total
        wall_pong[pl.ds(GROUP * o + EXT, EXT), :] = total
    for copy in span_first:
        copy.wait_recv()
    contract(PTS, 1, 0, load_faces, forward(2), dense(face_ping, GROUP))
    contract(EXT, 1, 0, strided(face_ping), forward(1), dense(face_pong, GROUP))

    def finish_body(g, carry):
        low = face_pong[pl.ds(g * (2 * GROUP), GROUP, stride=2), :]
        high = face_pong[pl.ds(g * (2 * GROUP) + 1, GROUP, stride=2), :]
        scale = halves(lambda b: jnp.where(left_lanes, vector(1, POINT[LOW], b), vector(1, POINT[HIGH], b)), g)
        for a in range(EXT):
            spot = pl.ds(pl.multiple_of(a * SLAB + g * GROUP, 8), GROUP)
            total = part[spot, :] + scale * wall_pong[pl.ds(GROUP * a, GROUP), :]
            total = total + vector(0, POINT[LOW], a) * low + vector(0, POINT[HIGH], a) * high
            part[spot, :] = total * divisor[spot, :]
        return carry

    lax.fori_loop(0, EXT // 2, finish_body, 0)
    def contract_small(pieces, coeff, outputs, store):
        for o in outputs:
            total = None
            for i in range(EXT):
                term = coeff(o, i) * pieces[i]
                total = term if total is None else total + term
            store(o, total)

    def entry(direction, point, mode):
        return vec[direction, point, pl.ds(mode, 1), :]

    def slabs(g):
        return [part[pl.ds(pl.multiple_of(a * SLAB + g * GROUP, 8), GROUP), :] for a in range(EXT)]

    def put_side(g, o, total):
        side_first[pl.ds(pl.multiple_of((o - PTS) * SLAB + g * GROUP, 8), GROUP), :] = total

    contract(EXT, EXT // 2, 0, slabs, backward(0), put_side, (LOW, HIGH))
    for side in range(2):
        def put_second(o, total):
            side_second[pl.ds(16 * o, EXT), :] = total

        def put_third(o, total):
            side_third[side, o, pl.ds(0, EXT), :] = total

        pieces = [side_first[pl.ds(side * SLAB + c, EXT, stride=EXT), :] for c in range(EXT)]
        contract_small(pieces, lambda o, i: entry(2, POINT[o], i), range(EXT), put_second)
        pieces = [side_second[pl.ds(b, EXT, stride=16), :] for b in range(EXT)]
        contract_small(pieces, lambda o, i: entry(1, POINT[o], i), range(PTS), put_third)
    span_second = [
        remote(side_third.at[1, :, inner, :], faces_out.at[0], span_send.at[2], span_recv.at[2], "span", above),
        remote(side_third.at[0, :, inner, :], faces_out.at[1], span_send.at[3], span_recv.at[3], "span", below),
    ]
    for copy in span_second:
        copy.start()

    def wall_first(a, carry):
        pieces = [part[pl.ds(a * SLAB + b * EXT, EXT), :] for b in range(EXT)]

        def put(o, total):
            wall_one[pl.ds((o - PTS) * SLAB + a * EXT, EXT), :] = total

        contract_small(pieces, lambda o, i: entry(1, POINT[o], i), (LOW, HIGH), put)
        return carry

    lax.fori_loop(0, EXT, wall_first, 0)
    contract(EXT, 1, 0, strided(wall_one), backward(2), dense(wall_two, GROUP))
    wall_three[pl.ds(PTS * GROUP, 16), :] = jnp.zeros((16, LANES), f32)
    contract(EXT, 1, 0, strided(wall_two), backward(0), dense(wall_three, GROUP), range(PTS))

    def wall_layer(t, half, layer):
        return wall_three[pl.ds(t * GROUP + 16 * half + (layer - PTS), 8, stride=2), :]

    pack(lambda t, half: wall_layer(t, half, HIGH), LANES - EZ, 2)
    pack(lambda t, half: wall_layer(t, half, LOW), 0, 3)
    send_walls(1)

    contract(EXT, EXT // 2, 0, strided(part), backward(2), dense(mixed))
    pl.when(s > 0)(coarse_solve)
    contract(EXT, EXT // 2, 0, strided(mixed), backward(1), dense(part), range(PTS))

    def place_points(g, o, total):
        solved[o, 2 * g, pl.ds(0, EXT), :] = total[0:EXT]
        solved[o, 2 * g + 1, pl.ds(0, EXT), :] = total[EXT:GROUP]

    contract(EXT, PTS // 2, 0, strided(part), backward(0), place_points, range(PTS))

    flat_solved = solved.reshape(PTS * EXT * 16, LANES)

    def stream_body(g, carry):
        def at(v):
            return pl.ds(g * (GROUP * 16) + v, GROUP, stride=16)
        low = jnp.where(inside, permute(flat_solved[at(HIGH), :], upstream), 0.0)
        high = jnp.where(inside, permute(flat_solved[at(LOW), :], downstream), 0.0)
        flat_solved[at(0), :] = flat_solved[at(0), :] + low
        flat_solved[at(PTS - 1), :] = flat_solved[at(PTS - 1), :] + high
        return carry

    lax.fori_loop(0, PTS // 2, stream_body, 0)

    def own_walls(t, carry):
        for half in range(2):
            span_rows = pl.ds(8 * half, 8)
            low = jnp.where(first_line, 0.0, turn(wall_layer(t, half, HIGH), EZ))
            high = jnp.where(end_line, 0.0, turn(wall_layer(t, half, LOW), -EZ))
            count = 8 if half == 0 else PTS - 8
            kept = pl.ds(8 * half, count)
            solved[t, 0, kept, :] = solved[t, 0, kept, :] + low[0:count]
            solved[t, PTS - 1, kept, :] = solved[t, PTS - 1, kept, :] + high[0:count]
        return carry

    lax.fori_loop(0, PTS, own_walls, 0)

    def out_copy(t):
        return pltpu.make_async_copy(solved.at[t, inner, inner, :], out.at[t], out_sem.at[t])

    for t in range(PTS):
        out_copy(t).start()
    index_copy.wait()

    @pl.when(jnp.logical_not(has_down))
    def _():
        no_neighbour(0).wait()

    @pl.when(jnp.logical_not(has_up))
    def _():
        no_neighbour(1).wait()

    receive_walls(1)
    for copy in span_second:
        copy.wait_recv()
    for k in range(1, walls):
        y_arrival(k).wait_recv()
    y_keep.wait()
    for copy in span_first + span_second:
        copy.wait_send()
    finish_walls(0)
    finish_walls(1)
    for k in range(1, walls):
        x_copy(k).wait_send()
        y_copy(k).wait_send()
    for t in range(PTS):
        out_copy(t).wait()


def unpack(packed, side, t, half, lane_to):
    slot = 2 * t + half
    part = packed[side, pl.ds(8 * (slot // 8), 8), :]
    return turn(part, lane_to - EZ * (slot % 8))


def lift(
    rows, verts, base, faces, packed, values, index, out,
    held, faces_here, packed_here, values_here, index_here, near, low_lift, step_lift, wall_add, in_sem, out_sem, small_sem,
):
    smalls = [
        pltpu.make_async_copy(there, here, small_sem.at[k])
        for k, (there, here) in enumerate((
            (index, index_here), (values, values_here), (packed, packed_here), (faces, faces_here)
        ))
    ]
    loads = [pltpu.make_async_copy(base.at[t], held.at[t], in_sem.at[t]) for t in range(PTS)]
    stores = [pltpu.make_async_copy(held.at[t], out.at[t], out_sem.at[t]) for t in range(PTS)]
    order = tuple(range(1, PTS - 1)) + (0, PTS - 1)
    for copy in smalls[:3] + [loads[t] for t in order[:-2]] + smalls[3:] + [loads[t] for t in order[-2:]]:
        copy.start()
    smalls[0].wait()
    width = 3 * LANES
    count = values_here.shape[0] * 8
    ids = index_here[pl.ds(0, 1), :]
    downstream8 = index_here[pl.ds(8, 8), pl.ds(0, LANES)]
    factor, shift = divider(rows, verts)
    known = jnp.maximum(ids, 0)
    owner = (known * factor) >> shift
    local = known - owner * rows
    wanted = owner * 8 + (local >> 7)
    picks = (rows_of((LANES, width)) == (local & (LANES - 1))).astype(f32).astype(jnp.bfloat16)
    smalls[2].wait()
    first_line = lanes_of((8, LANES)) < EZ
    end_line = lanes_of((8, LANES)) >= LANES - EZ
    for t in range(PTS):
        for half in range(2):
            kept = pl.ds(8 * half, 8)
            wall_add[0, t, kept, :] = jnp.where(first_line, unpack(packed_here, 0, t, half, 0), 0.0)
            wall_add[1, t, kept, :] = jnp.where(end_line, unpack(packed_here, 1, t, half, LANES - EZ), 0.0)
    smalls[1].wait()
    table = exact(values_here[...].reshape(count, LANES), picks, ((1,), (0,)))
    found = jnp.sum(jnp.where(rows_of((count, width)) == wanted, table, 0.0), axis=0, keepdims=True)
    last_line = lanes_of((1, LANES)) >= LANES - EZ
    tops = found[:, 2 * LANES :]
    top = (tops, turn(tops, EZ))
    near[...] = jnp.zeros(near.shape, f32)
    for a in range(2):
        row = found[:, a * LANES : (a + 1) * LANES]
        near[pl.ds(2 * a, 1), :] = row
        near[pl.ds(2 * a + 1, 1), :] = jnp.where(last_line, top[a], turn(row, -EZ))
    begins = near[...]
    ends = permute(begins, downstream8)
    share = (2.0 * rows_of((PTS, LANES)).astype(f32) + 1.0) / (2 * PTS)
    across = []
    for ab in range(4):
        begin = jnp.broadcast_to(begins[ab : ab + 1], (PTS, LANES))
        end = jnp.broadcast_to(ends[ab : ab + 1], (PTS, LANES))
        across.append(begin + (end - begin) * share)
    for u in range(PTS):
        low = across[0] + (across[1] - across[0]) * upper(u)
        high = across[2] + (across[3] - across[2]) * upper(u)
        low_lift[u] = low
        step_lift[u] = high - low
    for t in order:
        loads[t].wait()
        for u in range(PTS):
            held[t, u] = held[t, u] + (low_lift[u] + step_lift[u] * upper(t))
        held[t, 0] = held[t, 0] + wall_add[0, t, pl.ds(0, PTS), :]
        held[t, PTS - 1] = held[t, PTS - 1] + wall_add[1, t, pl.ds(0, PTS), :]
        if t in (0, PTS - 1):
            side = 0 if t == 0 else 1
            if t == 0:
                smalls[3].wait()
            for u in range(PTS):
                held[t, u] = held[t, u] + faces_here[side, u]
        stores[t].start()
    for copy in stores:
        copy.wait()


def solution(mesh):
    spans, walls = mesh.shape["span"], mesh.shape["wall"]

    def per_device(residual, eig_values, eig_vectors, corner_map, stream_links, coarse_inverse):
        rows, verts = coarse_inverse.shape[1:]
        held = -(-verts // LANES)
        held = -(-held // 8) * 8
        padded = -(-rows // LANES) * LANES
        vmem = lambda *shape: pltpu.VMEM(shape, f32)
        dma = lambda count: pltpu.SemaphoreType.DMA((count,))
        shapes = [
            jax.ShapeDtypeStruct(residual.shape, f32),
            jax.ShapeDtypeStruct((2, PTS, PTS, LANES), f32),
            jax.ShapeDtypeStruct((2, 24, LANES), f32),
            jax.ShapeDtypeStruct((walls, 8, LANES), f32),
            jax.ShapeDtypeStruct((16, 3 * LANES), jnp.int32),
        ]
        parts = pl.pallas_call(
            functools.partial(kernel, spans, walls, verts),
            out_shape=shapes,
            in_specs=[pl.BlockSpec(memory_space=pltpu.HBM)] * 6,
            out_specs=[pl.BlockSpec(memory_space=pl.ANY)] * 5,
            scratch_shapes=[
                vmem(PTS, EXT, 16, LANES),
                vmem(2, EXT, 16, LANES),
                vmem(PTS, 16, LANES),
                vmem(EXT * EXT * PTS, LANES),
                vmem(EXT * EXT * PTS, LANES),
                vmem(EXT * GROUP, LANES),
                vmem(EXT * GROUP, LANES),
                vmem(EXT * 16, LANES),
                vmem(EXT * GROUP, LANES),
                vmem(EXT * SLAB, LANES),
                vmem(EXT * SLAB, LANES),
                vmem(EXT * SLAB, LANES),
                vmem(2 * SLAB, LANES),
                vmem(EXT * 16, LANES),
                vmem(2, PTS, 16, LANES),
                vmem(2 * SLAB, LANES),
                vmem(EXT * GROUP, LANES),
                vmem(PTS * GROUP + 16, LANES),
                vmem(PTS, EXT, 16, LANES),
                vmem(*eig_vectors.shape),
                vmem(*eig_values.shape),
                pltpu.VMEM(corner_map.shape, jnp.int32),
                pltpu.SMEM(stream_links.shape, jnp.int32),
                vmem(rows, verts),
                vmem(2, padded, LANES),
                vmem(2, 8, LANES),
                vmem(held, LANES),
                vmem(walls, held, LANES),
                vmem(8, LANES),
                pltpu.VMEM((16, 3 * LANES), jnp.int32),
                vmem(4, 24, LANES),
                vmem(2, 24, LANES),
                dma(8), dma(PTS + 2), dma(4), dma(4), dma(4), dma(4),
                dma(walls), dma(walls), dma(walls), dma(walls),
                pltpu.SemaphoreType.REGULAR((2,)),
            ],
            compiler_params=pltpu.CompilerParams(
                collective_id=0, has_side_effects=True, vmem_limit_bytes=60 * 2**20
            ),
        )(residual, eig_values, eig_vectors, corner_map, stream_links, jnp.transpose(coarse_inverse, (1, 0, 2)))
        return pl.pallas_call(
            functools.partial(lift, rows, verts),
            out_shape=jax.ShapeDtypeStruct(residual.shape, f32),
            in_specs=[pl.BlockSpec(memory_space=pltpu.HBM)] * 5,
            out_specs=pl.BlockSpec(memory_space=pl.ANY),
            scratch_shapes=[
                vmem(*residual.shape),
                vmem(2, PTS, PTS, LANES),
                vmem(2, 24, LANES),
                vmem(walls, 8, LANES),
                pltpu.VMEM((16, 3 * LANES), jnp.int32),
                vmem(8, LANES),
                vmem(PTS, PTS, LANES),
                vmem(PTS, PTS, LANES),
                vmem(2, PTS, 16, LANES),
                dma(PTS), dma(PTS), dma(4),
            ],
            compiler_params=pltpu.CompilerParams(vmem_limit_bytes=60 * 2**20),
        )(*parts)

    return jax.shard_map(
        per_device,
        mesh=mesh,
        in_specs=(
            P(None, None, None, ("span", "wall")),
            P(None, None, ("span", "wall")),
            P(None, None, None, ("span", "wall")),
            P(None, ("span", "wall")),
            P(),
            P("span", "wall", None),
        ),
        out_specs=P(None, None, None, ("span", "wall")),
        check_vma=False,
    )
```

```python
import functools

import jax
import jax.numpy as jnp
from jax import lax
from jax.experimental import pallas as pl
from jax.experimental.pallas import tpu as pltpu
from jax.sharding import PartitionSpec as P

PTS = 10
EXT = 12
EY = 8
EZ = 16
LANES = 128
SLAB = EXT * EXT
GROUP = 2 * EXT
POINT = tuple(range(1, PTS + 1)) + (0, EXT - 1)
LOW, HIGH = PTS, PTS + 1
precise = lax.Precision.HIGHEST
f32 = jnp.float32


def upper(index):
    return (2 * index + 1) / (2 * PTS)


def rows_of(shape):
    return lax.broadcasted_iota(jnp.int32, shape, 0)


def lanes_of(shape):
    return lax.broadcasted_iota(jnp.int32, shape, 1)


def turn(values, shift):
    return pltpu.roll(values, shift % LANES, 1)


def permute(values, index):
    return jnp.take_along_axis(values, jnp.broadcast_to(index, values.shape), axis=1)


def exact(values, picks, dims, swapped=False):
    picks = picks.astype(jnp.bfloat16)
    total = None
    for _ in range(3):
        piece = values.astype(jnp.bfloat16)
        values = values - piece.astype(f32)
        pair = (picks, piece) if swapped else (piece, picks)
        term = lax.dot_general(*pair, (dims, ((), ())), preferred_element_type=f32)
        total = term if total is None else total + term
    return total


def divider(rows, top):
    for shift in range(12, 26):
        factor = -(-(1 << shift) // rows)
        if top * factor < 1 << 31 and all((v * factor) >> shift == v // rows for v in range(top)):
            return factor, shift
    raise ValueError("no divider")


def contract(count, groups, first, load, coeff, store, outputs=range(EXT)):
    def body(group, carry):
        pieces = load(group)
        for o in outputs:
            total = None
            for i in range(count):
                term = coeff(o, i) * pieces[i]
                total = term if total is None else total + term
            store(group, o, total)
        return carry

    lax.fori_loop(first, groups, body, 0)


def kernel(
    spans, walls, verts,
    res_in, val_in, vec_in, map_in, link_in, inv_in, out, faces_out, walls_out, yall, index_out,
    field, faces, wall_face, ping, pong, face_ping, face_pong, wall_ping, wall_pong, part, mixed, divisor,
    side_first, side_second, side_third, wall_one, wall_two, wall_three, solved,
    vec, val, cmap, links, inv, acc, csum, xown, xall, yown, index, pack_out, pack_in,
    local_sem, out_sem, span_send, span_recv, wall_send, wall_recv, x_send, x_recv, y_send, y_recv, meet,
):
    s = lax.axis_index("span")
    w = lax.axis_index("wall")
    rows = verts // walls
    tiles = verts // LANES
    rest = verts - tiles * LANES
    inner = pl.ds(0, PTS)

    load_field = pltpu.make_async_copy(res_in, field.at[inner, inner, inner, :], local_sem.at[0])
    load_map = pltpu.make_async_copy(map_in, cmap, local_sem.at[1])
    load_links = pltpu.make_async_copy(link_in, links, local_sem.at[2])
    load_vec = pltpu.make_async_copy(vec_in, vec, local_sem.at[3])
    load_val = pltpu.make_async_copy(val_in, val, local_sem.at[4])
    load_inv = pltpu.make_async_copy(inv_in.at[:, 0, :], inv, local_sem.at[5])
    for copy in (load_links, load_map, load_field, load_vec, load_val):
        copy.start()

    across_count = 4 if walls == 16 else 1
    along_count = walls // across_count
    row, column = lax.div(w, across_count), lax.rem(w, across_count)

    def partner(k, sign):
        down, right = k // across_count, k % across_count
        if sign < 0:
            down, right = along_count - down, across_count - right
        return lax.rem(row + down, along_count) * across_count + lax.rem(column + right, across_count)

    def hops(k):
        down, right = k // across_count, k % across_count
        return min(down, along_count - down) + min(right, across_count - right)

    partners = sorted(range(1, walls), key=lambda k: -hops(k))

    above = lax.rem(s + 1, spans)
    below = lax.rem(s + spans - 1, spans)
    even = lax.rem(s, 2) == 0
    hears_above = jnp.logical_or(even, s == spans - 1)
    hears_below = jnp.logical_and(even, s > 0)
    speaks_above = jnp.logical_not(hears_above)
    speaks_below = jnp.logical_not(hears_below)
    early = jnp.logical_or(row + column < 3, s < spans - 1)
    barrier = pltpu.get_barrier_semaphore()
    for k in partners:
        pl.semaphore_signal(barrier, inc=1, device_id={"wall": partner(k, 1)})

    @pl.when(speaks_above)
    def _():
        pl.semaphore_signal(barrier, inc=1, device_id={"span": above})

    @pl.when(speaks_below)
    def _():
        pl.semaphore_signal(barrier, inc=1, device_id={"span": below})

    def remote(src, dst, send, recv, axis, peer):
        return pltpu.make_async_remote_copy(
            src_ref=src, dst_ref=dst, send_sem=send, recv_sem=recv, device_id={axis: peer}
        )

    span_first = [
        remote(res_in.at[PTS - 1], faces.at[0, inner, inner, :], span_send.at[0], span_recv.at[0], "span", above),
        remote(res_in.at[0], faces.at[1, inner, inner, :], span_send.at[1], span_recv.at[1], "span", below),
    ]
    def wall_copies(turn_index):
        base = 2 * turn_index
        landing = walls_out if turn_index else pack_in
        up = remote(pack_out.at[base], landing.at[0], wall_send.at[base], wall_recv.at[base],
                    "wall", lax.rem(w + 1, walls))
        down = remote(pack_out.at[base + 1], landing.at[1], wall_send.at[base + 1], wall_recv.at[base + 1],
                      "wall", lax.rem(w + walls - 1, walls))
        return up, down

    has_up = w < walls - 1
    has_down = w > 0

    def send_walls(turn_index):
        up, down = wall_copies(turn_index)
        pl.when(has_up)(up.start)
        pl.when(has_down)(down.start)

    def receive_walls(turn_index):
        up, down = wall_copies(turn_index)
        pl.when(has_down)(up.wait_recv)
        pl.when(has_up)(down.wait_recv)

    def finish_walls(turn_index):
        up, down = wall_copies(turn_index)
        pl.when(has_up)(up.wait_send)
        pl.when(has_down)(down.wait_send)

    lane = lanes_of((8, LANES))
    slot_of = lane // EZ

    def pack(source, lane_from, dest):
        parts = [None] * 3
        for t in range(PTS):
            for half in range(2):
                slot = 2 * t + half
                piece = source(t, half)
                place = slot % 8
                moved = turn(piece, EZ * place - lane_from)
                held = parts[slot // 8]
                parts[slot // 8] = moved if held is None else jnp.where(slot_of == place, moved, held)
        for index, part in enumerate(parts):
            pack_out[dest, pl.ds(8 * index, 8), :] = part

    def no_neighbour(side):
        return pltpu.make_async_copy(pack_in.at[side], walls_out.at[side], out_sem.at[PTS + side])

    @pl.when(jnp.logical_not(has_down))
    def _():
        pack_in[0] = jnp.zeros(pack_in.shape[1:], f32)
        no_neighbour(0).start()

    @pl.when(jnp.logical_not(has_up))
    def _():
        pack_in[1] = jnp.zeros(pack_in.shape[1:], f32)
        no_neighbour(1).start()

    blank = jnp.zeros((16 - PTS, LANES), f32)
    for t in range(PTS):
        field[t, 0, pl.ds(PTS, 16 - PTS), :] = blank
        field[t, PTS - 1, pl.ds(PTS, 16 - PTS), :] = blank
    for side in range(2):
        for u in (LOW, HIGH):
            faces[side, u] = jnp.zeros((16, LANES), f32)
    csum[...] = jnp.zeros(csum.shape, f32)
    acc[...] = jnp.zeros(acc.shape, f32)

    load_links.wait()
    lane_row = lanes_of((8, LANES))
    place = lane_row % EZ
    up_slot = jnp.zeros((8, LANES), jnp.int32)
    down_slot = jnp.zeros((8, LANES), jnp.int32)
    for q in range(EZ):
        up_slot = jnp.where(place == q, links[0, q], up_slot)
        down_slot = jnp.where(place == q, links[1, q], down_slot)
    line = lane_row - place
    upstream8 = line + up_slot
    downstream8 = line + down_slot
    upstream = jnp.concatenate([upstream8] * 3, axis=0)
    downstream = jnp.concatenate([downstream8] * 3, axis=0)

    load_field.wait()
    pack(lambda t, half: field[t, PTS - 1, pl.ds(8 * half, 8), :], LANES - EZ, 0)
    pack(lambda t, half: field[t, 0, pl.ds(8 * half, 8), :], 0, 1)
    used = pl.ds(0, tiles + (1 if rest else 0))
    width = 3 * LANES
    index_copy = pltpu.make_async_copy(index, index_out, local_sem.at[6])

    def vertex_sums():
        def corner_body(u, sums):
            total = None
            weighted = None
            for t in range(PTS):
                piece = field[t, u, inner, :]
                term = piece * upper(t)
                total = piece if total is None else total + piece
                weighted = term if weighted is None else weighted + term
            low = total - weighted
            share = (2.0 * u.astype(f32) + 1.0) / (2 * PTS)
            low_up = low * share
            high_up = weighted * share
            return (sums[0] + (low - low_up), sums[1] + low_up,
                    sums[2] + (weighted - high_up), sums[3] + high_up)

        nothing = jnp.zeros((PTS, LANES), f32)
        sums = lax.fori_loop(0, PTS, corner_body, (nothing,) * 4)
        share_v = (2.0 * rows_of((PTS, LANES)).astype(f32) + 1.0) / (2 * PTS)
        for ab in range(4):
            upper_part = sums[ab] * share_v
            csum[0, pl.ds(ab, 1), :] = jnp.sum(sums[ab] - upper_part, axis=0, keepdims=True)
            csum[1, pl.ds(ab, 1), :] = jnp.sum(upper_part, axis=0, keepdims=True)
        lines = csum[0] + permute(csum[1], upstream8)
        moved_up = jnp.where(lane >= EZ, turn(lines, EZ), 0.0)
        moved_down = turn(lines, -EZ)
        lane1 = lanes_of((1, LANES))
        last_line = lane1 >= LANES - EZ
        second_line = lane1 >= LANES - 2 * EZ
        values = jnp.concatenate([
            lines[0:1] + moved_up[1:2],
            lines[2:3] + moved_up[3:4],
            jnp.where(last_line, lines[1:2], jnp.where(second_line, moved_down[3:4], 0.0)),
        ], axis=1)

        load_map.wait()
        moved_map = turn(cmap[...], -EZ)
        ids = jnp.concatenate([
            cmap[0:1, :],
            cmap[4:5, :],
            jnp.where(last_line, cmap[2:3, :], jnp.where(second_line, moved_map[6:7], -1)),
        ], axis=1)
        index[pl.ds(0, 8), :] = jnp.broadcast_to(ids, (8, width))
        index[pl.ds(8, 8), :] = jnp.concatenate([downstream8] * 3, axis=1)
        index_copy.start()
        held = xown.shape[0]
        spread = jnp.where(rows_of((held, width)) == (ids >> 7), values, 0.0)
        onehot = (rows_of((LANES, width)) == (ids & (LANES - 1))).astype(f32)
        xown[...] = exact(spread, onehot, ((1,), (1,)))

    pl.when(early)(vertex_sums)

    greeted = walls - 1 + hears_above.astype(jnp.int32) + hears_below.astype(jnp.int32)
    pl.semaphore_wait(barrier, greeted)
    send_walls(0)

    @pl.when(hears_above)
    def _():
        pl.semaphore_signal(meet.at[1], inc=1, device_id={"span": above})

    @pl.when(hears_below)
    def _():
        pl.semaphore_signal(meet.at[0], inc=1, device_id={"span": below})

    pl.when(jnp.logical_not(early))(vertex_sums)

    def x_copy(k):
        return remote(xown.at[used], xall.at[k, used], x_send.at[k], x_recv.at[k], "wall", partner(k, 1))

    for k in partners:
        x_copy(k).start()
    pl.when(hears_above)(span_first[0].start)
    pl.when(hears_below)(span_first[1].start)
    load_inv.start()

    first_line = lane < EZ
    end_line = lane >= LANES - EZ

    def wall_body(t, carry):
        for half in range(2):
            span_rows = pl.ds(8 * half, 8)
            low = turn(field[t, PTS - 1, span_rows, :], EZ)
            field[t, LOW, span_rows, :] = jnp.where(first_line, 0.0, low)
            high = turn(field[t, 0, span_rows, :], -EZ)
            field[t, HIGH, span_rows, :] = jnp.where(end_line, 0.0, high)
        return carry

    lax.fori_loop(0, PTS, wall_body, 0)

    @pl.when(speaks_above)
    def _():
        pl.semaphore_wait(meet.at[0], 1)
        span_first[0].start()

    @pl.when(jnp.logical_not(even))
    def _():
        pl.semaphore_wait(meet.at[1], 1)
        span_first[1].start()

    def vector(direction, point, mode):
        return jnp.broadcast_to(vec[direction, point, pl.ds(mode, 1), :], (GROUP, LANES))

    def strided(ref, count=EXT):
        return lambda g: [ref[pl.ds(g * (GROUP * count) + i, GROUP, stride=count), :] for i in range(count)]

    def dense(ref, length=SLAB):
        def put(g, o, total):
            ref[pl.ds(pl.multiple_of(o * length + g * GROUP, 8), GROUP), :] = total
        return put

    load_vec.wait()
    load_val.wait()
    flat_field = field.reshape(PTS * EXT * 16, LANES)
    flat_faces = faces.reshape(2 * EXT * 16, LANES)
    inside = (rows_of((GROUP, LANES)) % EXT) < PTS

    def load_first(g):
        pieces = [flat_field[pl.ds(g * (GROUP * 16) + v, GROUP, stride=16), :] for v in range(PTS)]
        pieces.append(jnp.where(inside, permute(pieces[PTS - 1], upstream), 0.0))
        pieces.append(jnp.where(inside, permute(pieces[0], downstream), 0.0))
        return pieces

    def load_faces(g):
        return [flat_faces[pl.ds(v, GROUP, stride=16), :] for v in range(PTS)]

    forward = lambda d: lambda o, i: vector(d, POINT[i], o)
    backward = lambda d: lambda o, i: vector(d, POINT[o], i)
    short = EXT * PTS
    contract(EXT, PTS // 2, 0, load_first, forward(2), dense(ping, short))
    contract(EXT, PTS // 2, 0, strided(ping), forward(1), dense(pong, short))
    contract(PTS, EXT // 2, 0, strided(pong, PTS), forward(0), dense(part))

    second_half = rows_of((GROUP, LANES)) >= EXT
    left_lanes = lanes_of((GROUP, LANES)) < LANES // 2
    third = jnp.concatenate([val[2], val[2]], axis=0)

    def halves(pick, g):
        return jnp.where(second_half, pick(2 * g + 1), pick(2 * g))

    def divisor_body(g, carry):
        both = third + halves(lambda b: jnp.broadcast_to(val[1, pl.ds(b, 1), :], (GROUP, LANES)), g)
        for a in range(EXT):
            spot = pl.ds(pl.multiple_of(a * SLAB + g * GROUP, 8), GROUP)
            divisor[spot, :] = 1.0 / (jnp.broadcast_to(val[0, pl.ds(a, 1), :], (GROUP, LANES)) + both)
        return carry

    lax.fori_loop(0, EXT // 2, divisor_body, 0)

    @pl.when(s == 0)
    def _():
        pl.semaphore_wait(meet.at[1], 1)
        span_first[1].start()

    y_keep = pltpu.make_async_copy(yown, yall.at[w], local_sem.at[7])

    def y_copy(k):
        return remote(yown, yall.at[w], y_send.at[k], y_recv.at[k], "wall", partner(k, 1))

    def y_arrival(k):
        sender = partner(k, -1)
        return remote(yown, yall.at[sender], y_send.at[k], y_recv.at[k], "wall", sender)

    def coarse_solve():
        load_inv.wait()
        for k in range(1, walls):
            x_copy(k).wait_recv()
        total_x = xown[...]
        for k in range(1, walls):
            total_x = total_x + xall[k]
        xall[0] = total_x

        def times(start, count, ways):
            sums = [None] * ways
            for c in range(tiles):
                term = inv[pl.ds(start, count), pl.ds(c * LANES, LANES)] * xall[0, pl.ds(c, 1), :]
                held = sums[c % ways]
                sums[c % ways] = term if held is None else held + term
            total = sums[0]
            for part_sum in sums[1:]:
                total = total + part_sum
            acc[0, pl.ds(start, count), :] = total
            if rest:
                tail = inv[pl.ds(start, count), pl.ds(tiles * LANES, rest)] * xall[0, pl.ds(tiles, 1), pl.ds(0, rest)]
                acc[1, pl.ds(start, count), pl.ds(0, rest)] = tail

        chunk = 64
        whole = rows // chunk

        def times_body(r, carry):
            times(pl.multiple_of(r * chunk, chunk), chunk, 2)
            return carry

        lax.fori_loop(0, whole, times_body, 0)
        if rows - whole * chunk:
            times(whole * chunk, rows - whole * chunk, 8)
        ones = jnp.ones((8, LANES), f32)
        own = exact(acc[0] + acc[1], ones, ((1,), (1,)), True)
        row8 = rows_of((8, LANES))
        tile = own[:, 0:LANES]
        for part in range(1, acc.shape[1] // LANES):
            tile = jnp.where(row8 == part, own[:, part * LANES : (part + 1) * LANES], tile)
        yown[...] = tile
        y_keep.start()

        for k in partners:
            y_copy(k).start()

    pl.when(s == 0)(coarse_solve)

    receive_walls(0)
    for t in range(PTS):
        for half in range(2):
            kept = jnp.where(end_line, unpack(pack_in, 1, t, half, LANES - EZ), 0.0)
            wall_face[t, pl.ds(8 * half, 8), :] = jnp.where(first_line, unpack(pack_in, 0, t, half, 0), kept)
    flat_wall = wall_face.reshape(PTS * 16, LANES)
    pieces = [flat_wall[pl.ds(v, PTS, stride=16), :] for v in range(PTS)]
    for o in range(EXT):
        total = None
        for v in range(PTS):
            term = vec[2, POINT[v], pl.ds(o, 1), :] * pieces[v]
            total = term if total is None else total + term
        wall_ping[pl.ds(16 * o, PTS), :] = total
    pieces = [wall_ping[pl.ds(t, EXT, stride=16), :] for t in range(PTS)]
    for o in range(EXT):
        total = None
        for t in range(PTS):
            term = vec[0, POINT[t], pl.ds(o, 1), :] * pieces[t]
            total = term if total is None else total + term
        wall_pong[pl.ds(GROUP * o, EXT), :] = total
        wall_pong[pl.ds(GROUP * o + EXT, EXT), :] = total
    for copy in span_first:
        copy.wait_recv()
    contract(PTS, 1, 0, load_faces, forward(2), dense(face_ping, GROUP))
    contract(EXT, 1, 0, strided(face_ping), forward(1), dense(face_pong, GROUP))

    def finish_body(g, carry):
        low = face_pong[pl.ds(g * (2 * GROUP), GROUP, stride=2), :]
        high = face_pong[pl.ds(g * (2 * GROUP) + 1, GROUP, stride=2), :]
        scale = halves(lambda b: jnp.where(left_lanes, vector(1, POINT[LOW], b), vector(1, POINT[HIGH], b)), g)
        for a in range(EXT):
            spot = pl.ds(pl.multiple_of(a * SLAB + g * GROUP, 8), GROUP)
            total = part[spot, :] + scale * wall_pong[pl.ds(GROUP * a, GROUP), :]
            total = total + vector(0, POINT[LOW], a) * low + vector(0, POINT[HIGH], a) * high
            part[spot, :] = total * divisor[spot, :]
        return carry

    lax.fori_loop(0, EXT // 2, finish_body, 0)
    def contract_small(pieces, coeff, outputs, store):
        for o in outputs:
            total = None
            for i in range(EXT):
                term = coeff(o, i) * pieces[i]
                total = term if total is None else total + term
            store(o, total)

    def entry(direction, point, mode):
        return vec[direction, point, pl.ds(mode, 1), :]

    def slabs(g):
        return [part[pl.ds(pl.multiple_of(a * SLAB + g * GROUP, 8), GROUP), :] for a in range(EXT)]

    def put_side(g, o, total):
        side_first[pl.ds(pl.multiple_of((o - PTS) * SLAB + g * GROUP, 8), GROUP), :] = total

    contract(EXT, EXT // 2, 0, slabs, backward(0), put_side, (LOW, HIGH))
    for side in range(2):
        def put_second(o, total):
            side_second[pl.ds(16 * o, EXT), :] = total

        def put_third(o, total):
            side_third[side, o, pl.ds(0, EXT), :] = total

        pieces = [side_first[pl.ds(side * SLAB + c, EXT, stride=EXT), :] for c in range(EXT)]
        contract_small(pieces, lambda o, i: entry(2, POINT[o], i), range(EXT), put_second)
        pieces = [side_second[pl.ds(b, EXT, stride=16), :] for b in range(EXT)]
        contract_small(pieces, lambda o, i: entry(1, POINT[o], i), range(PTS), put_third)
    span_second = [
        remote(side_third.at[1, :, inner, :], faces_out.at[0], span_send.at[2], span_recv.at[2], "span", above),
        remote(side_third.at[0, :, inner, :], faces_out.at[1], span_send.at[3], span_recv.at[3], "span", below),
    ]
    for copy in span_second:
        copy.start()

    def wall_first(a, carry):
        pieces = [part[pl.ds(a * SLAB + b * EXT, EXT), :] for b in range(EXT)]

        def put(o, total):
            wall_one[pl.ds((o - PTS) * SLAB + a * EXT, EXT), :] = total

        contract_small(pieces, lambda o, i: entry(1, POINT[o], i), (LOW, HIGH), put)
        return carry

    lax.fori_loop(0, EXT, wall_first, 0)
    contract(EXT, 1, 0, strided(wall_one), backward(2), dense(wall_two, GROUP))
    wall_three[pl.ds(PTS * GROUP, 16), :] = jnp.zeros((16, LANES), f32)
    contract(EXT, 1, 0, strided(wall_two), backward(0), dense(wall_three, GROUP), range(PTS))

    def wall_layer(t, half, layer):
        return wall_three[pl.ds(t * GROUP + 16 * half + (layer - PTS), 8, stride=2), :]

    pack(lambda t, half: wall_layer(t, half, HIGH), LANES - EZ, 2)
    pack(lambda t, half: wall_layer(t, half, LOW), 0, 3)
    send_walls(1)

    contract(EXT, EXT // 2, 0, strided(part), backward(2), dense(mixed))
    pl.when(s > 0)(coarse_solve)
    contract(EXT, EXT // 2, 0, strided(mixed), backward(1), dense(part), range(PTS))

    def place_points(g, o, total):
        solved[o, 2 * g, pl.ds(0, EXT), :] = total[0:EXT]
        solved[o, 2 * g + 1, pl.ds(0, EXT), :] = total[EXT:GROUP]

    contract(EXT, PTS // 2, 0, strided(part), backward(0), place_points, range(PTS))

    flat_solved = solved.reshape(PTS * EXT * 16, LANES)

    def stream_body(g, carry):
        def at(v):
            return pl.ds(g * (GROUP * 16) + v, GROUP, stride=16)
        low = jnp.where(inside, permute(flat_solved[at(HIGH), :], upstream), 0.0)
        high = jnp.where(inside, permute(flat_solved[at(LOW), :], downstream), 0.0)
        flat_solved[at(0), :] = flat_solved[at(0), :] + low
        flat_solved[at(PTS - 1), :] = flat_solved[at(PTS - 1), :] + high
        return carry

    lax.fori_loop(0, PTS // 2, stream_body, 0)

    def own_walls(t, carry):
        for half in range(2):
            span_rows = pl.ds(8 * half, 8)
            low = jnp.where(first_line, 0.0, turn(wall_layer(t, half, HIGH), EZ))
            high = jnp.where(end_line, 0.0, turn(wall_layer(t, half, LOW), -EZ))
            count = 8 if half == 0 else PTS - 8
            kept = pl.ds(8 * half, count)
            solved[t, 0, kept, :] = solved[t, 0, kept, :] + low[0:count]
            solved[t, PTS - 1, kept, :] = solved[t, PTS - 1, kept, :] + high[0:count]
        return carry

    lax.fori_loop(0, PTS, own_walls, 0)

    def out_copy(t):
        return pltpu.make_async_copy(solved.at[t, inner, inner, :], out.at[t], out_sem.at[t])

    for t in range(PTS):
        out_copy(t).start()
    index_copy.wait()

    @pl.when(jnp.logical_not(has_down))
    def _():
        no_neighbour(0).wait()

    @pl.when(jnp.logical_not(has_up))
    def _():
        no_neighbour(1).wait()

    receive_walls(1)
    for copy in span_second:
        copy.wait_recv()
    for k in range(1, walls):
        y_arrival(k).wait_recv()
    y_keep.wait()
    for copy in span_first + span_second:
        copy.wait_send()
    finish_walls(0)
    finish_walls(1)
    for k in range(1, walls):
        x_copy(k).wait_send()
        y_copy(k).wait_send()
    for t in range(PTS):
        out_copy(t).wait()


def unpack(packed, side, t, half, lane_to):
    slot = 2 * t + half
    part = packed[side, pl.ds(8 * (slot // 8), 8), :]
    return turn(part, lane_to - EZ * (slot % 8))


def lift(
    rows, verts, base, faces, packed, values, index, out,
    held, faces_here, packed_here, values_here, index_here, near, low_lift, step_lift, wall_add, in_sem, out_sem, small_sem,
):
    smalls = [
        pltpu.make_async_copy(there, here, small_sem.at[k])
        for k, (there, here) in enumerate((
            (index, index_here), (values, values_here), (packed, packed_here), (faces, faces_here)
        ))
    ]
    loads = [pltpu.make_async_copy(base.at[t], held.at[t], in_sem.at[t]) for t in range(PTS)]
    stores = [pltpu.make_async_copy(held.at[t], out.at[t], out_sem.at[t]) for t in range(PTS)]
    order = tuple(range(1, PTS - 1)) + (0, PTS - 1)
    for copy in smalls[:3] + [loads[t] for t in order[:-2]] + smalls[3:] + [loads[t] for t in order[-2:]]:
        copy.start()
    smalls[0].wait()
    width = 3 * LANES
    count = values_here.shape[0] * 8
    ids = index_here[pl.ds(0, 1), :]
    downstream8 = index_here[pl.ds(8, 8), pl.ds(0, LANES)]
    factor, shift = divider(rows, verts)
    known = jnp.maximum(ids, 0)
    owner = (known * factor) >> shift
    local = known - owner * rows
    wanted = owner * 8 + (local >> 7)
    picks = (rows_of((LANES, width)) == (local & (LANES - 1))).astype(f32).astype(jnp.bfloat16)
    smalls[2].wait()
    first_line = lanes_of((8, LANES)) < EZ
    end_line = lanes_of((8, LANES)) >= LANES - EZ
    for t in range(PTS):
        for half in range(2):
            kept = pl.ds(8 * half, 8)
            wall_add[0, t, kept, :] = jnp.where(first_line, unpack(packed_here, 0, t, half, 0), 0.0)
            wall_add[1, t, kept, :] = jnp.where(end_line, unpack(packed_here, 1, t, half, LANES - EZ), 0.0)
    smalls[1].wait()
    table = exact(values_here[...].reshape(count, LANES), picks, ((1,), (0,)))
    found = jnp.sum(jnp.where(rows_of((count, width)) == wanted, table, 0.0), axis=0, keepdims=True)
    last_line = lanes_of((1, LANES)) >= LANES - EZ
    tops = found[:, 2 * LANES :]
    top = (tops, turn(tops, EZ))
    near[...] = jnp.zeros(near.shape, f32)
    for a in range(2):
        row = found[:, a * LANES : (a + 1) * LANES]
        near[pl.ds(2 * a, 1), :] = row
        near[pl.ds(2 * a + 1, 1), :] = jnp.where(last_line, top[a], turn(row, -EZ))
    begins = near[...]
    ends = permute(begins, downstream8)
    share = (2.0 * rows_of((PTS, LANES)).astype(f32) + 1.0) / (2 * PTS)
    across = []
    for ab in range(4):
        begin = jnp.broadcast_to(begins[ab : ab + 1], (PTS, LANES))
        end = jnp.broadcast_to(ends[ab : ab + 1], (PTS, LANES))
        across.append(begin + (end - begin) * share)
    for u in range(PTS):
        low = across[0] + (across[1] - across[0]) * upper(u)
        high = across[2] + (across[3] - across[2]) * upper(u)
        low_lift[u] = low
        step_lift[u] = high - low
    for t in order:
        loads[t].wait()
        for u in range(PTS):
            held[t, u] = held[t, u] + (low_lift[u] + step_lift[u] * upper(t))
        held[t, 0] = held[t, 0] + wall_add[0, t, pl.ds(0, PTS), :]
        held[t, PTS - 1] = held[t, PTS - 1] + wall_add[1, t, pl.ds(0, PTS), :]
        if t in (0, PTS - 1):
            side = 0 if t == 0 else 1
            if t == 0:
                smalls[3].wait()
            for u in range(PTS):
                held[t, u] = held[t, u] + faces_here[side, u]
        stores[t].start()
    for copy in stores:
        copy.wait()


def solution(mesh):
    spans, walls = mesh.shape["span"], mesh.shape["wall"]

    def per_device(residual, eig_values, eig_vectors, corner_map, stream_links, coarse_inverse):
        rows, verts = coarse_inverse.shape[1:]
        held = -(-verts // LANES)
        held = -(-held // 8) * 8
        padded = -(-rows // LANES) * LANES
        vmem = lambda *shape: pltpu.VMEM(shape, f32)
        dma = lambda count: pltpu.SemaphoreType.DMA((count,))
        shapes = [
            jax.ShapeDtypeStruct(residual.shape, f32),
            jax.ShapeDtypeStruct((2, PTS, PTS, LANES), f32),
            jax.ShapeDtypeStruct((2, 24, LANES), f32),
            jax.ShapeDtypeStruct((walls, 8, LANES), f32),
            jax.ShapeDtypeStruct((16, 3 * LANES), jnp.int32),
        ]
        parts = pl.pallas_call(
            functools.partial(kernel, spans, walls, verts),
            out_shape=shapes,
            in_specs=[pl.BlockSpec(memory_space=pltpu.HBM)] * 6,
            out_specs=[pl.BlockSpec(memory_space=pl.ANY)] * 5,
            scratch_shapes=[
                vmem(PTS, EXT, 16, LANES),
                vmem(2, EXT, 16, LANES),
                vmem(PTS, 16, LANES),
                vmem(EXT * EXT * PTS, LANES),
                vmem(EXT * EXT * PTS, LANES),
                vmem(EXT * GROUP, LANES),
                vmem(EXT * GROUP, LANES),
                vmem(EXT * 16, LANES),
                vmem(EXT * GROUP, LANES),
                vmem(EXT * SLAB, LANES),
                vmem(EXT * SLAB, LANES),
                vmem(EXT * SLAB, LANES),
                vmem(2 * SLAB, LANES),
                vmem(EXT * 16, LANES),
                vmem(2, PTS, 16, LANES),
                vmem(2 * SLAB, LANES),
                vmem(EXT * GROUP, LANES),
                vmem(PTS * GROUP + 16, LANES),
                vmem(PTS, EXT, 16, LANES),
                vmem(*eig_vectors.shape),
                vmem(*eig_values.shape),
                pltpu.VMEM(corner_map.shape, jnp.int32),
                pltpu.SMEM(stream_links.shape, jnp.int32),
                vmem(rows, verts),
                vmem(2, padded, LANES),
                vmem(2, 8, LANES),
                vmem(held, LANES),
                vmem(walls, held, LANES),
                vmem(8, LANES),
                pltpu.VMEM((16, 3 * LANES), jnp.int32),
                vmem(4, 24, LANES),
                vmem(2, 24, LANES),
                dma(8), dma(PTS + 2), dma(4), dma(4), dma(4), dma(4),
                dma(walls), dma(walls), dma(walls), dma(walls),
                pltpu.SemaphoreType.REGULAR((2,)),
            ],
            compiler_params=pltpu.CompilerParams(
                collective_id=0, has_side_effects=True, vmem_limit_bytes=60 * 2**20
            ),
        )(residual, eig_values, eig_vectors, corner_map, stream_links, jnp.transpose(coarse_inverse, (1, 0, 2)))
        return pl.pallas_call(
            functools.partial(lift, rows, verts),
            out_shape=jax.ShapeDtypeStruct(residual.shape, f32),
            in_specs=[pl.BlockSpec(memory_space=pltpu.HBM)] * 5,
            out_specs=pl.BlockSpec(memory_space=pl.ANY),
            scratch_shapes=[
                vmem(*residual.shape),
                vmem(2, PTS, PTS, LANES),
                vmem(2, 24, LANES),
                vmem(walls, 8, LANES),
                pltpu.VMEM((16, 3 * LANES), jnp.int32),
                vmem(8, LANES),
                vmem(PTS, PTS, LANES),
                vmem(PTS, PTS, LANES),
                vmem(2, PTS, 16, LANES),
                dma(PTS), dma(PTS), dma(4),
            ],
            compiler_params=pltpu.CompilerParams(vmem_limit_bytes=60 * 2**20),
        )(*parts)

    return jax.shard_map(
        per_device,
        mesh=mesh,
        in_specs=(
            P(None, None, None, ("span", "wall")),
            P(None, None, ("span", "wall")),
            P(None, None, None, ("span", "wall")),
            P(None, ("span", "wall")),
            P(),
            P("span", "wall", None),
        ),
        out_specs=P(None, None, None, ("span", "wall")),
        check_vma=False,
    )
```
